512 devices in a mesh: seg: 16 (over z, y_lo), dp: 32 (over y_hi, x, core).
Axes of the slice: x: 4, y: 8 (y_hi: 4, y_lo: 2; y = y_hi * 2 + y_lo), z: 8, core: 2. Of those that a mesh axis runs over, the one named last changes fastest.
Arguments:
- tokens: bfloat16 [32, 2048, 1024], P('dp', 'seg'), may hold values from -6 to 6
- grad_output: bfloat16 [32, 2048, 1024], P('dp', 'seg'), may hold values from -6 to 6
- memories: bfloat16 [32, 16, 32, 1024], P('dp', 'seg'), may hold values from -6 to 6
- grad_last: bfloat16 [32, 32, 1024], P('dp'), may hold values from -6 to 6
- norm_gain: float32 [1024], replicated, may hold values from 0.1 to 1.9
- query_weight: bfloat16 [1024, 1024], P('dp'), may hold values from -0.1875 to 0.1875
- key_weight: bfloat16 [1024, 256], P('dp'), may hold values from -0.1875 to 0.1875
- value_weight: bfloat16 [1024, 256], P('dp'), may hold values from -0.1875 to 0.1875
- out_weight: bfloat16 [1024, 1024], P(None, 'dp'), may hold values from -0.1875 to 0.1875
Outputs:
- grad_tokens: bfloat16 [32, 2048, 1024], P('dp', 'seg')
- grad_memories: bfloat16 [32, 16, 32, 1024], P('dp', 'seg')
- grad_key: float32 [1024, 256], P('dp')
- grad_value: float32 [1024, 256], P('dp')
The draws below stay inside these ranges and needn't reach their ends.
All inputs are finite; a program needn't handle non-finite values.
Results may differ from the reference program's by a relative error of at most 0.035.
Values may be sent and summed in bfloat16 or wider, within the bound.
No kernel may reach another device: no remote copies, remote signals or barrier semaphores. Data moves between devices by JAX's collectives and lax.ppermute only.
A program may use at most 64 MiB of HBM per device.

```python
import math
import jax
import jax.numpy as jnp
from jax import lax

D = 1024
HEADS = 16
KV_HEADS = 4
HEAD_DIM = 64
MEMORY = 32
SEG_TOKENS = 128
QUERY_WIDTH = 1024
KV_WIDTH = 256
DOCS = 32
DOC_TOKENS = 2048
N_SEG = 16


def with_spikes(result, key, source, target, blocks, factor):
    owner, partner = [(jnp.arange(result.shape[axis_at]) // (result.shape[axis_at] // blocks)).reshape([-1 if axis == axis_at else 1 for axis in range(result.ndim)]) for axis_at in (source, target)]
    chosen = jax.random.permutation(key, blocks)[partner]
    strong = (owner == chosen) | (owner == (partner + blocks // 2) % blocks)
    return jnp.where(strong, factor * result, result)


def steps_of(stream_key, shape, pieces, smallest, largest):
    factor_of, own = 1.0, jax.random.fold_in(stream_key, 6)
    for dim, shards_of in pieces:
        draws = jnp.exp(jax.random.uniform(jax.random.fold_in(own, dim), (shards_of,), jnp.float32, smallest / len(pieces), largest / len(pieces)))
        factor_of = factor_of * jnp.repeat(draws, shape[dim] // shards_of).reshape([-1 if axis == dim else 1 for axis in range(len(shape))])
    return factor_of


def bell_draw(rng, dims, scale, limit, pieces=(), dtype=jnp.bfloat16):
    factor_of = steps_of(rng, dims, pieces, -0.22, 0.18) if pieces else 1.0
    result = jax.random.normal(rng, dims, jnp.float32) * scale * factor_of
    return jnp.minimum(jnp.maximum(result, -limit), limit).astype(dtype)


def gaussian_with(key, dims, scale, reach, shards, heavy, kind=jnp.bfloat16):
    array = scale * jax.random.normal(key, dims, jnp.float32)
    if shards:
        array = array * steps_of(key, dims, shards, -0.22, 0.18)
    return jnp.clip(with_spikes(array, jax.random.fold_in(key, 3), *heavy), -reach, reach).astype(kind)


def setup_inputs(seed: int = 0) -> dict:
    streams_of = jax.random.split(jax.random.key(seed), 10)
    tokens = gaussian_with(streams_of[0], (DOCS, DOC_TOKENS, D), 1.0, 6.0, ((0, 32), (1, 16)), (0, 2, 32, 2.75))
    grad_output = bell_draw(streams_of[1], (DOCS, DOC_TOKENS, D), 1.0, 6.0, ((0, 32), (1, 16)))
    memories = bell_draw(streams_of[2], (DOCS, N_SEG, MEMORY, D), 1.0, 6.0, ((0, 32), (1, 16)))
    grad_last = bell_draw(streams_of[3], (DOCS, MEMORY, D), 1.0, 6.0, ((0, 32),))
    norm_gain = jnp.clip(1.0 + 0.18 * jax.random.normal(streams_of[4], (D,), jnp.float32), 0.1, 1.9)
    query_weight = bell_draw(streams_of[5], (D, QUERY_WIDTH), D ** -0.5, 0.1875, ((0, 32),))
    key_weight = bell_draw(streams_of[6], (D, KV_WIDTH), D ** -0.5, 0.1875, ((0, 32),))
    value_weight = bell_draw(streams_of[7], (D, KV_WIDTH), D ** -0.5, 0.1875, ((0, 32),))
    out_weight = bell_draw(streams_of[8], (QUERY_WIDTH, D), QUERY_WIDTH ** -0.5, 0.1875, ((1, 32),))
    return {"tokens": tokens, "grad_output": grad_output, "memories": memories, "grad_last": grad_last, "norm_gain": norm_gain, "query_weight": query_weight, "key_weight": key_weight, "value_weight": value_weight, "out_weight": out_weight}


epsilon = 1e-05

def widen(value):
    return lax.optimization_barrier(value).astype(jnp.float32)

def segment_backward(memory_rows, token_rows, memory_cotangent, token_cotangent, norm_gain, query_weight, key_weight, value_weight, out_weight):
    group_size = HEADS // KV_HEADS
    score_scale = 1.0 / math.sqrt(HEAD_DIM)
    hidden = jnp.concatenate([memory_rows.astype(jnp.float32), token_rows.astype(jnp.float32)], axis=0)
    total_rows = hidden.shape[0]
    inverse_norm = lax.rsqrt(lax.optimization_barrier(jnp.mean(hidden * hidden, axis=-1, keepdims=True)) + epsilon)
    normed = (hidden * inverse_norm * norm_gain).astype(jnp.bfloat16)
    queries = jnp.dot(normed, query_weight, preferred_element_type=jnp.float32).astype(jnp.bfloat16)
    key_rows = jnp.dot(normed, key_weight, preferred_element_type=jnp.float32).astype(jnp.bfloat16)
    value_rows = jnp.dot(normed, value_weight, preferred_element_type=jnp.float32).astype(jnp.bfloat16)
    query_heads = widen(queries).reshape(total_rows, KV_HEADS, group_size, HEAD_DIM)
    key_heads = widen(key_rows).reshape(total_rows, KV_HEADS, HEAD_DIM)
    value_heads = widen(value_rows).reshape(total_rows, KV_HEADS, HEAD_DIM)
    scores = jnp.einsum('igad,jgd->gaij', query_heads, key_heads) * score_scale
    row_index = lax.broadcasted_iota(jnp.int32, (total_rows, total_rows), 0)
    column_index = lax.broadcasted_iota(jnp.int32, (total_rows, total_rows), 1)
    allowed = (row_index < MEMORY) | (column_index <= row_index)
    raised = jnp.where(allowed, jnp.exp(scores), 0.0)
    softmax_full = raised / lax.optimization_barrier(jnp.sum(raised, axis=-1, keepdims=True))
    softmax_half = softmax_full.astype(jnp.bfloat16)
    cotangent = jnp.concatenate([memory_cotangent, token_cotangent], axis=0)
    upstream = jnp.dot(cotangent, out_weight.T, preferred_element_type=jnp.float32).astype(jnp.bfloat16)
    upstream_heads = widen(upstream).reshape(total_rows, KV_HEADS, group_size, HEAD_DIM)
    prob_grad = jnp.einsum('igad,jgd->gaij', upstream_heads, value_heads)
    centred = prob_grad - lax.optimization_barrier(jnp.sum(softmax_full * prob_grad, axis=-1, keepdims=True))
    score_grad = widen((softmax_full * centred * score_scale).astype(jnp.bfloat16))
    query_grad = jnp.einsum('gaij,jgd->igad', score_grad, key_heads).reshape(total_rows, -1).astype(jnp.bfloat16)
    key_grad = jnp.einsum('gaij,igad->jgd', score_grad, query_heads).reshape(total_rows, -1).astype(jnp.bfloat16)
    value_grad = jnp.einsum('gaij,igad->jgd', widen(softmax_half), upstream_heads).reshape(total_rows, -1).astype(jnp.bfloat16)
    normed_grad = jnp.dot(query_grad, query_weight.T, preferred_element_type=jnp.float32)
    normed_grad = normed_grad + jnp.dot(key_grad, key_weight.T, preferred_element_type=jnp.float32)
    normed_grad = normed_grad + jnp.dot(value_grad, value_weight.T, preferred_element_type=jnp.float32)
    scaled_grad = normed_grad * norm_gain
    hidden_grad = cotangent.astype(jnp.float32) + inverse_norm * (scaled_grad - hidden * inverse_norm * inverse_norm * lax.optimization_barrier(jnp.mean(scaled_grad * hidden, axis=-1, keepdims=True)))
    key_update = jnp.dot(normed.T, key_grad, preferred_element_type=jnp.float32)
    value_update = jnp.dot(normed.T, value_grad, preferred_element_type=jnp.float32)
    return (hidden_grad[:MEMORY].astype(jnp.bfloat16), hidden_grad[MEMORY:].astype(jnp.bfloat16), key_update, value_update)

def reference(tokens, grad_output, memories, grad_last, norm_gain, query_weight, key_weight, value_weight, out_weight):
    documents = tokens.shape[0]
    token_blocks = tokens.reshape(documents, N_SEG, SEG_TOKENS, D).transpose(1, 0, 2, 3)
    grad_blocks = grad_output.reshape(documents, N_SEG, SEG_TOKENS, D).transpose(1, 0, 2, 3)
    memory_blocks = memories.transpose(1, 0, 2, 3)
    batched = jax.vmap(segment_backward, in_axes=(0, 0, 0, 0, None, None, None, None, None))

    def backward_step(carried, inputs):
        following, key_total, value_total = carried
        memory_rows, token_rows, token_cotangent = inputs
        memory_grad, token_grad, key_update, value_update = batched(memory_rows, token_rows, following, token_cotangent, norm_gain, query_weight, key_weight, value_weight, out_weight)
        return ((memory_grad, key_total + lax.optimization_barrier(jnp.sum(key_update, axis=0)), value_total + lax.optimization_barrier(jnp.sum(value_update, axis=0))), (memory_grad, token_grad))
    initial = (grad_last, jnp.zeros((D, KV_WIDTH), jnp.float32), jnp.zeros((D, KV_WIDTH), jnp.float32))
    finished, stacked = lax.scan(backward_step, initial, (memory_blocks, token_blocks, grad_blocks), reverse=True)
    grad_memories = stacked[0].transpose(1, 0, 2, 3)
    grad_tokens = stacked[1].transpose(1, 0, 2, 3).reshape(documents, DOC_TOKENS, D)
    return (grad_tokens, grad_memories, finished[1] / DOCS, finished[2] / DOCS)
```

```python
import functools

import jax
import jax.numpy as jnp
from jax import lax
from jax.experimental import pallas as pl
from jax.experimental.pallas import tpu as pltpu
from jax.sharding import PartitionSpec as P

D = 1024
GROUPS = 4
PER_GROUP = 4
HEAD = 64
WIDE = PER_GROUP * HEAD
KV = GROUPS * HEAD
MEM = 32
TOK = 128
ROWS = MEM + TOK
SPAN = 4
EPS = 1e-05
SCALE = 0.125
BF = jnp.bfloat16
F32 = jnp.float32


def nn(a, b):
    return lax.dot_general(a, b, (((1,), (0,)), ((), ())), preferred_element_type=F32)


def nt(a, b):
    return lax.dot_general(a, b, (((1,), (1,)), ((), ())), preferred_element_type=F32)


def tn(a, b):
    return lax.dot_general(a, b, (((0,), (0,)), ((), ())), preferred_element_type=F32)


def normalised(rows, gain):
    inverse = lax.rsqrt(jnp.mean(rows * rows, axis=-1, keepdims=True) + EPS)
    return inverse, (rows * inverse * gain).astype(BF)


def norm_backward(cotangent, normed_grad, hidden, inverse, gain):
    scaled = normed_grad * gain
    mean = jnp.mean(scaled * hidden, axis=-1, keepdims=True)
    return cotangent + inverse * (scaled - hidden * (inverse * inverse * mean))


def repeated(rows, g):
    half = rows[:, (g // 2) * 128 : (g // 2) * 128 + 128].astype(F32)
    lane = lax.broadcasted_iota(jnp.int32, half.shape, 1)
    kept = jnp.where((lane < HEAD) == (g % 2 == 0), half, 0.0)
    both = kept + pltpu.roll(kept, HEAD, 1)
    return jnp.concatenate([both, both], axis=1).astype(BF)


def stacked(rows):
    rows = rows.astype(F32)
    lane = lax.broadcasted_iota(jnp.int32, rows.shape, 1) // HEAD
    return jnp.concatenate([jnp.where(lane == a, rows, 0.0) for a in range(PER_GROUP)], axis=0).astype(BF)


def unstacked(rows):
    n = rows.shape[0] // PER_GROUP
    lane = lax.broadcasted_iota(jnp.int32, (n, WIDE), 1) // HEAD
    total = jnp.zeros((n, WIDE), F32)
    for a in range(PER_GROUP):
        total = jnp.where(lane == a, rows[a * n : (a + 1) * n], total)
    return total


def folded(parts):
    sums = []
    for part in parts:
        half = part[:, :128] + part[:, 128:]
        sums.append(half + pltpu.roll(half, HEAD, 1))
    lane = lax.broadcasted_iota(jnp.int32, sums[0].shape, 1)
    return jnp.concatenate(
        [jnp.where(lane < HEAD, sums[0], sums[1]), jnp.where(lane < HEAD, sums[2], sums[3])], axis=1
    )


def softmax_grad(probs, prob_grad):
    centred = prob_grad - jnp.sum(probs * prob_grad, axis=0, keepdims=True)
    return (probs * centred * SCALE).astype(BF)


def token_kernel(mem, tok, gout, gain, w, normed_out, qg_out, part_out, kvp_out, wt_out):
    hidden = jnp.concatenate([mem[...].astype(F32), tok[...].astype(F32)], axis=0)
    _, normed = normalised(hidden, gain[...])
    normed_out[...] = normed
    q = nn(normed[MEM:], w[:, :D])
    kv = nn(normed, w[:, D : D + 2 * KV]).astype(BF)
    up = nn(gout[...], w[:, D + 2 * KV :])
    k, v = kv[:, :KV], kv[:, KV:]
    key_at = lax.broadcasted_iota(jnp.int32, (ROWS, PER_GROUP * TOK), 0)
    row_at = lax.broadcasted_iota(jnp.int32, (ROWS, PER_GROUP * TOK), 1) % TOK
    seen = key_at <= row_at + MEM
    key_parts, value_parts = [], []
    for g in range(GROUPS):
        cols = slice(g * WIDE, (g + 1) * WIDE)
        zq = stacked(q[:, cols])
        zu = stacked(up[:, cols])
        krep, vrep = repeated(k, g), repeated(v, g)
        raised = jnp.where(seen, jnp.exp(nt(krep, zq) * SCALE), 0.0)
        probs = raised * (1.0 / jnp.sum(raised, axis=0, keepdims=True))
        score_grad = softmax_grad(probs, nt(vrep, zu))
        key_parts.append(nn(score_grad, zq))
        value_parts.append(nn(probs.astype(BF), zu))
        qg_out[:, cols] = unstacked(tn(score_grad, krep)).astype(BF)
    part = jnp.concatenate([folded(key_parts), folded(value_parts)], axis=1)
    part_out[...] = part
    kvp_out[:MEM, :] = part[:MEM].astype(BF)
    kvp_out[MEM:, :] = kv[MEM:]
    wt_out[...] = w[:, : D + 2 * KV].T


def ready_kernel(mem4, gain, w, kvp4, probs_out, krep_out, vrep_out, zq_out):
    _, normed = normalised(mem4[...].astype(F32), gain[...])
    qkv = nn(normed, w[:, : D + 2 * KV])
    for s in range(SPAN):
        rows = slice(s * MEM, (s + 1) * MEM)
        later = slice(s * ROWS + MEM, (s + 1) * ROWS)
        k = jnp.concatenate([qkv[rows, D : D + KV].astype(BF), kvp4[later, :KV]], axis=0)
        v = jnp.concatenate([qkv[rows, D + KV :].astype(BF), kvp4[later, KV:]], axis=0)
        for g in range(GROUPS):
            zq = stacked(qkv[rows, g * WIDE : (g + 1) * WIDE])
            krep = repeated(k, g)
            raised = jnp.exp(nt(krep, zq) * SCALE)
            at = s * GROUPS + g
            probs_out[at] = raised * (1.0 / jnp.sum(raised, axis=0, keepdims=True))
            krep_out[at] = krep
            vrep_out[at] = repeated(v, g)
            zq_out[at] = zq


def chain_kernel(fresh, arrived, held, mem4, gain, wo, wt, probs, krep, vrep, zq, kvp4, out):
    start = jnp.where(fresh[0] == 1, arrived[...].astype(F32), held[...].astype(F32)).astype(BF)
    out[SPAN * MEM :, :] = start
    current = start
    for s in reversed(range(SPAN)):
        rows = slice(s * MEM, (s + 1) * MEM)
        hidden = mem4[rows, :].astype(F32)
        inverse, _ = normalised(hidden, gain[...])
        up = nn(current, wo[...])
        query_grads, key_parts, value_parts = [], [], []
        for g in range(GROUPS):
            at = s * GROUPS + g
            zu = stacked(up[:, g * WIDE : (g + 1) * WIDE])
            p = probs[at]
            score_grad = softmax_grad(p, nt(vrep[at], zu))
            query_grads.append(unstacked(tn(score_grad, krep[at])))
            key_parts.append(nn(score_grad[:MEM], zq[at]))
            value_parts.append(nn(p[:MEM].astype(BF), zu))
        own = kvp4[s * ROWS : s * ROWS + MEM, :].astype(F32)
        kv_grad = jnp.concatenate([folded(key_parts), folded(value_parts)], axis=1) + own
        grads = jnp.concatenate(query_grads + [kv_grad], axis=1).astype(BF)
        current = norm_backward(current.astype(F32), nn(grads, wt[...]), hidden, inverse, gain[...]).astype(BF)
        out[rows, :] = current


def weight_kernel(place, chain, wo, probs, krep, vrep, zq, part, normed, kv_out, grad_out):
    r = place[0]
    current = chain[pl.ds(pl.multiple_of((r + 1) * MEM, MEM), MEM), :]
    up = nn(current, wo[...])
    key_parts, value_parts = [], []
    for g in range(GROUPS):
        at = r * GROUPS + g
        zu = stacked(up[:, g * WIDE : (g + 1) * WIDE])
        p = probs[at]
        score_grad = softmax_grad(p, nt(vrep[at], zu))
        key_parts.append(nn(score_grad, zq[at]))
        value_parts.append(nn(p.astype(BF), zu))
    kv_grad = jnp.concatenate([folded(key_parts), folded(value_parts)], axis=1) + part[...]
    kv_grad = kv_grad.astype(BF)
    kv_out[...] = kv_grad
    grad_out[...] = tn(normed[...], kv_grad).astype(BF)


def rows_kernel(tok, gout, gain, wt, qg, kv_grad, out):
    hidden = tok[...].astype(F32)
    inverse, _ = normalised(hidden, gain[...])
    normed_grad = nn(qg[...], wt[:D, :]) + nn(kv_grad[MEM:, :], wt[D:, :])
    out[...] = norm_backward(gout[...].astype(F32), normed_grad, hidden, inverse, gain[...]).astype(BF)


def call(kernel, outs, args, flops, scalars=0):
    vmem = pl.BlockSpec(memory_space=pltpu.VMEM)
    smem = pl.BlockSpec(memory_space=pltpu.SMEM)
    moved = sum(a.size * a.dtype.itemsize for a in args) + sum(o.size * o.dtype.itemsize for o in outs)
    return pl.pallas_call(
        kernel,
        out_shape=outs,
        in_specs=[smem] * scalars + [vmem] * (len(args) - scalars),
        out_specs=[vmem] * len(outs),
        compiler_params=pltpu.CompilerParams(vmem_limit_bytes=48 * 1024 * 1024),
        cost_estimate=pl.CostEstimate(flops=flops, bytes_accessed=moved, transcendentals=0),
    )(*args)


def shape(dims, dtype=BF):
    return jax.ShapeDtypeStruct(dims, dtype)


def runs(axis_size, length, stride):
    block = length * stride
    return [
        [b + o + i * stride for i in range(length)] for b in range(0, axis_size, block) for o in range(stride)
    ]


def shared_out(block, length, stride):
    groups = runs(lax.axis_size("dp"), length, stride)
    got = lax.all_to_all(block, "dp", 0, 0, tiled=True, axis_index_groups=groups)
    got = got.reshape((length, block.shape[0] // length) + block.shape[1:])
    return jnp.sum(got.astype(F32), axis=0).astype(BF)


def summed(block, length, stride):
    groups = runs(lax.axis_size("seg"), length, stride)
    got = lax.all_gather(block, "seg", axis=0, axis_index_groups=groups)
    return jnp.sum(got.astype(F32), axis=0)


def reduced(grad):
    docs = lax.axis_size("dp")
    rows = D // docs
    core = lax.axis_index("dp") % 2
    halves = grad.reshape(docs // 2, 2, rows, 2 * KV)
    mine = lax.dynamic_index_in_dim(halves, core, 1, keepdims=False)
    other = lax.dynamic_index_in_dim(halves, 1 - core, 1, keepdims=False)
    got = lax.ppermute(other, "dp", [(i, i ^ 1) for i in range(docs)])
    block = (mine.astype(F32) + got.astype(F32)).astype(BF)
    if docs == 32:
        block = block.reshape(4, 4, rows, 2 * KV)
        block = shared_out(block, 4, 8)[0]
        block = shared_out(block, 4, 2)[0]
    else:
        block = block[0]
    block = summed(block, 4, 1).astype(BF)
    return summed(block, lax.axis_size("seg") // 4, 4)


def body(tokens, grad_output, memories, grad_last, norm_gain, query_weight, key_weight, value_weight, out_weight):
    position = lax.axis_index("seg")
    n_seg = lax.axis_size("seg")
    turns = n_seg // SPAN
    tok, gout, mem, gain = tokens[0], grad_output[0], memories[0, 0], norm_gain[None]

    shard = jnp.concatenate([query_weight, key_weight, value_weight, out_weight.T], axis=1)
    w = lax.all_gather(shard, "dp", axis=0, tiled=True)
    near = runs(n_seg, SPAN, 1)
    mem4 = lax.all_gather(mem, "seg", axis=0, tiled=True, axis_index_groups=near)

    normed, qg, part, kvp, wt = call(
        token_kernel,
        [shape((ROWS, D)), shape((TOK, D)), shape((ROWS, 2 * KV), F32), shape((ROWS, 2 * KV)), shape((D + 2 * KV, D))],
        (mem, tok, gout, gain, w),
        1_500_000_000,
    )
    kvp4 = lax.all_gather(kvp, "seg", axis=0, tiled=True, axis_index_groups=near)
    count = SPAN * GROUPS
    probs, krep, vrep, zq = call(
        ready_kernel,
        [
            shape((count, ROWS, PER_GROUP * MEM), F32),
            shape((count, ROWS, WIDE)),
            shape((count, ROWS, WIDE)),
            shape((count, PER_GROUP * MEM, WIDE)),
        ],
        (mem4, gain, w, kvp4),
        800_000_000,
    )
    wo = w[:, D + 2 * KV :]
    block = position // SPAN
    held = grad_last[0]
    arrived = held
    for turn in range(turns):
        fresh = (block == turns - 1 - turn).astype(jnp.int32)[None]
        (chain,) = call(
            chain_kernel,
            [shape(((SPAN + 1) * MEM, D))],
            (fresh, arrived, held, mem4, gain, wo, wt, probs, krep, vrep, zq, kvp4),
            1_000_000_000,
            scalars=1,
        )
        held = chain[SPAN * MEM :]
        if turn < turns - 1:
            route = [(i, i - SPAN) for i in range((turns - 1 - turn) * SPAN, (turns - turn) * SPAN)]
            arrived = lax.ppermute(chain[:MEM], "seg", route)
    place = (position % SPAN)[None].astype(jnp.int32)
    kv_grad, grad = call(
        weight_kernel,
        [shape((ROWS, 2 * KV)), shape((D, 2 * KV))],
        (place, chain, wo, probs, krep, vrep, zq, part, normed),
        400_000_000,
        scalars=1,
    )
    (grad_tokens,) = call(
        rows_kernel, [shape((TOK, D))], (tok, gout, gain, wt, qg, kv_grad), 500_000_000
    )
    grad_memories = lax.dynamic_slice_in_dim(chain, place[0] * MEM, MEM, 0)
    total = reduced(grad) / lax.axis_size("dp")
    return (grad_tokens[None], grad_memories[None, None], total[:, :KV], total[:, KV:])


def solution(mesh):
    in_specs = (
        P("dp", "seg", None),
        P("dp", "seg", None),
        P("dp", "seg", None, None),
        P("dp", None, None),
        P(),
        P("dp", None),
        P("dp", None),
        P("dp", None),
        P(None, "dp"),
    )
    out_specs = (P("dp", "seg", None), P("dp", "seg", None, None), P("dp", None), P("dp", None))
    return jax.shard_map(body, mesh=mesh, in_specs=in_specs, out_specs=out_specs, check_vma=False)
```

```python
import functools

import jax
import jax.numpy as jnp
from jax import lax
from jax.experimental import pallas as pl
from jax.experimental.pallas import tpu as pltpu
from jax.sharding import PartitionSpec as P

D = 1024
GROUPS = 4
PER_GROUP = 4
HEAD = 64
WIDE = PER_GROUP * HEAD
KV = GROUPS * HEAD
MEM = 32
TOK = 128
ROWS = MEM + TOK
SPAN = 4
EPS = 1e-05
SCALE = 0.125
BF = jnp.bfloat16
F32 = jnp.float32


def nn(a, b):
    return lax.dot_general(a, b, (((1,), (0,)), ((), ())), preferred_element_type=F32)


def nt(a, b):
    return lax.dot_general(a, b, (((1,), (1,)), ((), ())), preferred_element_type=F32)


def tn(a, b):
    return lax.dot_general(a, b, (((0,), (0,)), ((), ())), preferred_element_type=F32)


def normalised(rows, gain):
    inverse = lax.rsqrt(jnp.mean(rows * rows, axis=-1, keepdims=True) + EPS)
    return inverse, (rows * inverse * gain).astype(BF)


def norm_backward(cotangent, normed_grad, hidden, inverse, gain):
    scaled = normed_grad * gain
    mean = jnp.mean(scaled * hidden, axis=-1, keepdims=True)
    return cotangent + inverse * (scaled - hidden * (inverse * inverse * mean))


def repeated(rows, g):
    half = rows[:, (g // 2) * 128 : (g // 2) * 128 + 128].astype(F32)
    lane = lax.broadcasted_iota(jnp.int32, half.shape, 1)
    kept = jnp.where((lane < HEAD) == (g % 2 == 0), half, 0.0)
    both = kept + pltpu.roll(kept, HEAD, 1)
    return jnp.concatenate([both, both], axis=1).astype(BF)


def stacked(rows):
    rows = rows.astype(F32)
    lane = lax.broadcasted_iota(jnp.int32, rows.shape, 1) // HEAD
    return jnp.concatenate([jnp.where(lane == a, rows, 0.0) for a in range(PER_GROUP)], axis=0).astype(BF)


def unstacked(rows):
    n = rows.shape[0] // PER_GROUP
    lane = lax.broadcasted_iota(jnp.int32, (n, WIDE), 1) // HEAD
    total = jnp.zeros((n, WIDE), F32)
    for a in range(PER_GROUP):
        total = jnp.where(lane == a, rows[a * n : (a + 1) * n], total)
    return total


def folded(parts):
    sums = []
    for part in parts:
        half = part[:, :128] + part[:, 128:]
        sums.append(half + pltpu.roll(half, HEAD, 1))
    lane = lax.broadcasted_iota(jnp.int32, sums[0].shape, 1)
    return jnp.concatenate(
        [jnp.where(lane < HEAD, sums[0], sums[1]), jnp.where(lane < HEAD, sums[2], sums[3])], axis=1
    )


def centred(scores_sum_axis, probs, products):
    total = jnp.sum(products, axis=scores_sum_axis, keepdims=True)
    return ((products - probs * total) * SCALE).astype(BF)


def group_columns(g):
    return slice(g * WIDE, (g + 1) * WIDE)


def token_kernel(mem, tok, gout, gain, w, normed_out, qg_out, part_out, kvp_out, wt_out):
    hidden = jnp.concatenate([mem[...].astype(F32), tok[...].astype(F32)], axis=0)
    _, normed = normalised(hidden, gain[...])
    normed_out[...] = normed
    q = nn(normed[MEM:], w[:, :D])
    kv = nn(normed, w[:, D : D + 2 * KV]).astype(BF)
    up = nn(gout[...], w[:, D + 2 * KV :])
    k, v = kv[:, :KV], kv[:, KV:]
    key_at = lax.broadcasted_iota(jnp.int32, (ROWS, PER_GROUP * TOK), 0)
    row_at = lax.broadcasted_iota(jnp.int32, (ROWS, PER_GROUP * TOK), 1) % TOK
    seen = key_at <= row_at + MEM
    key_parts, value_parts = [], []
    for g in range(GROUPS):
        cols = group_columns(g)
        zq = stacked(q[:, cols])
        zu = stacked(up[:, cols])
        krep, vrep = repeated(k, g), repeated(v, g)
        raised = jnp.where(seen, jnp.exp(nt(krep, zq) * SCALE), 0.0)
        probs = raised * (1.0 / jnp.sum(raised, axis=0, keepdims=True))
        score_grad = centred(0, probs, probs * nt(vrep, zu))
        key_parts.append(nn(score_grad, zq))
        value_parts.append(nn(probs.astype(BF), zu))
        qg_out[:, cols] = unstacked(tn(score_grad, krep)).astype(BF)
    part = jnp.concatenate([folded(key_parts), folded(value_parts)], axis=1)
    part_out[...] = part
    for copy in range(SPAN):
        kvp_out[copy * ROWS : copy * ROWS + MEM, :] = part[:MEM].astype(BF)
        kvp_out[copy * ROWS + MEM : (copy + 1) * ROWS, :] = kv[MEM:]
    wt_out[...] = w[:, : D + 2 * KV].T


def mix_kernel(mem4, last, gain, w, wt, mixed_out, qkv_out, hw_out, inv_out, u_out):
    inverse, normed = normalised(mem4[...].astype(F32), gain[...])
    inv_out[...] = inverse
    hw_out[...] = nn(mem4[...], w[:, D + 2 * KV :])
    qkv_out[...] = nn(normed, w[:, : D + 2 * KV])
    u_out[...] = nn(last[...], w[:, D + 2 * KV :]).astype(BF)
    scaled = (wt[...].astype(F32) * gain[...]).astype(BF)
    mixed_out[...] = nn(scaled, w[:, D + 2 * KV :]).astype(BF)


def ready_kernel(qkv4, kvp4, probs_k_out, probs_q_out, krep_out, vrep_out, zq_out):
    for s in range(SPAN):
        rows = slice(s * MEM, (s + 1) * MEM)
        later = slice(s * ROWS + MEM, (s + 1) * ROWS)
        k = jnp.concatenate([qkv4[rows, D : D + KV].astype(BF), kvp4[later, :KV]], axis=0)
        v = jnp.concatenate([qkv4[rows, D + KV :].astype(BF), kvp4[later, KV:]], axis=0)
        zqs = [stacked(qkv4[rows, group_columns(g)]) for g in range(GROUPS)]
        kreps = [repeated(k, g) for g in range(GROUPS)]
        raised_k = [jnp.exp(nt(krep, zq) * SCALE) for krep, zq in zip(kreps, zqs)]
        raised_q = [jnp.exp(nt(zq, krep) * SCALE) for krep, zq in zip(kreps, zqs)]
        for g in range(GROUPS):
            at = s * GROUPS + g
            probs_k_out[at] = raised_k[g] * (1.0 / jnp.sum(raised_k[g], axis=0, keepdims=True))
            probs_q_out[at] = raised_q[g] * (1.0 / jnp.sum(raised_q[g], axis=1, keepdims=True))
            krep_out[at] = kreps[g]
            vrep_out[at] = repeated(v, g)
            zq_out[at] = zqs[g]


def chain_kernel(
    latched, fresh, arrived, before, mixed, probs_k, probs_q, krep, vrep, zq, qkv4, hw4, inv4, kvp4, send_out, u_out, grads_out
):
    up = arrived[...].astype(F32)
    if latched:
        up = jnp.where(fresh[0] == 1, up, before[(SPAN - 1) * MEM :, :].astype(F32))
    for s in reversed(range(SPAN)):
        rows = slice(s * MEM, (s + 1) * MEM)
        u_out[rows, :] = up.astype(BF)
        ats = range(s * GROUPS, (s + 1) * GROUPS)
        zus = [stacked(up[:, group_columns(g)]) for g in range(GROUPS)]
        by_query = [probs_q[at] * nt(zu, vrep[at]) for at, zu in zip(ats, zus)]
        by_key = [probs_k[at] * nt(vrep[at], zu) for at, zu in zip(ats, zus)]
        value_parts = [nn(probs_k[at, :MEM].astype(BF), zu) for at, zu in zip(ats, zus)]
        score_grads = [centred(1, probs_q[at], products) for at, products in zip(ats, by_query)]
        totals = [jnp.sum(products, axis=0, keepdims=True) for products in by_key]
        near_grads = [
            ((products[:MEM] - probs_k[at, :MEM] * total) * SCALE).astype(BF)
            for at, products, total in zip(ats, by_key, totals)
        ]
        query_grads = [unstacked(nn(grad, krep[at])) for at, grad in zip(ats, score_grads)]
        key_parts = [nn(grad, zq[at]) for at, grad in zip(ats, near_grads)]
        own = kvp4[s * ROWS : s * ROWS + MEM, :].astype(F32)
        kv_grad = jnp.concatenate([folded(key_parts), folded(value_parts)], axis=1) + own
        grads = jnp.concatenate(query_grads + [kv_grad], axis=1).astype(BF)
        grads_out[rows, :] = grads
        inverse = inv4[rows, :]
        along = jnp.sum(grads.astype(F32) * qkv4[rows, :], axis=-1, keepdims=True) * (inverse * inverse / D)
        up = up + inverse * nn(grads, mixed[...]) - along * hw4[rows, :]
    send_out[...] = up.astype(BF)


def weight_kernel(place, u4, probs, krep, vrep, zq, part, normed, kv_out, mine_out, other_out):
    r = place[0]
    up = u4[pl.ds(pl.multiple_of(r * MEM, MEM), MEM), :]
    ats = [r * GROUPS + g for g in range(GROUPS)]
    zus = [stacked(up[:, group_columns(g)]) for g in range(GROUPS)]
    ps = [probs[at] for at in ats]
    products = [p * nt(vrep[at], zu) for at, p, zu in zip(ats, ps, zus)]
    value_parts = [nn(p.astype(BF), zu) for p, zu in zip(ps, zus)]
    score_grads = [centred(0, p, product) for p, product in zip(ps, products)]
    key_parts = [nn(grad, zq[at]) for at, grad in zip(ats, score_grads)]
    kv_grad = jnp.concatenate([folded(key_parts), folded(value_parts)], axis=1) + part[...]
    kv_grad = kv_grad.astype(BF)
    kv_out[...] = kv_grad
    share = mine_out.shape[1]
    grad = tn(normed[...], kv_grad).reshape(mine_out.shape[0], 2, share, 2 * KV)
    first = place[1] == 0
    mine_out[...] = jnp.where(first, grad[:, 0], grad[:, 1]).astype(BF)
    other_out[...] = jnp.where(first, grad[:, 1], grad[:, 0]).astype(BF)


def memory_kernel(place, grads4, wt, mem4, inv4, gain, own_out, all_out):
    hidden, inverse = mem4[...].astype(F32), inv4[...]
    change = norm_backward(0.0, nn(grads4[...], wt[...]), hidden, inverse, gain[...])
    total = jnp.zeros((MEM, D), F32)
    own = jnp.zeros((MEM, D), F32)
    for s in reversed(range(SPAN)):
        total = total + change[s * MEM : (s + 1) * MEM]
        own = jnp.where(place[0] == s, total, own)
    own_out[...] = own
    for copy in range(all_out.shape[0]):
        all_out[copy] = total.astype(BF)


def rows_kernel(tok, gout, gain, wt, qg, kv_grad, out):
    hidden = tok[...].astype(F32)
    inverse, _ = normalised(hidden, gain[...])
    normed_grad = nn(qg[...], wt[:D, :]) + nn(kv_grad[MEM:, :], wt[D:, :])
    out[...] = norm_backward(gout[...].astype(F32), normed_grad, hidden, inverse, gain[...]).astype(BF)


def call(kernel, outs, args, flops, scalars=0):
    vmem = pl.BlockSpec(memory_space=pltpu.VMEM)
    smem = pl.BlockSpec(memory_space=pltpu.SMEM)
    moved = sum(a.size * a.dtype.itemsize for a in args) + sum(o.size * o.dtype.itemsize for o in outs)
    return pl.pallas_call(
        kernel,
        out_shape=outs,
        in_specs=[smem] * scalars + [vmem] * (len(args) - scalars),
        out_specs=[vmem] * len(outs),
        compiler_params=pltpu.CompilerParams(vmem_limit_bytes=20 * 1024 * 1024),
        cost_estimate=pl.CostEstimate(flops=flops, bytes_accessed=moved, transcendentals=0),
    )(*args)


def shape(dims, dtype=BF):
    return jax.ShapeDtypeStruct(dims, dtype)


def runs(axis_size, length, stride):
    block = length * stride
    return [
        [b + o + i * stride for i in range(length)] for b in range(0, axis_size, block) for o in range(stride)
    ]


def spread(block, axis, groups):
    return lax.all_to_all(block, axis, 0, 0, tiled=True, axis_index_groups=groups)


def reduced(mine, other):
    docs, n_seg = lax.axis_size("dp"), lax.axis_size("seg")
    got = lax.ppermute(other, "dp", [(i, i ^ 1) for i in range(docs)])
    block = (mine.astype(F32) + got.astype(F32)).astype(BF)
    if docs > 2:
        block = lax.all_to_all(block, "dp", 0, 0, tiled=True, axis_index_groups=runs(docs, docs // 2, 2))
    block = jnp.sum(block.astype(F32), axis=0).astype(BF)
    for length, stride in ((SPAN, 1), (n_seg // SPAN, SPAN)):
        copies = jnp.broadcast_to(block[None], (length,) + block.shape)
        got = spread(copies, "seg", runs(n_seg, length, stride))
        total = jnp.sum(got.astype(F32), axis=0)
        block = total.astype(BF)
    return total


def body(tokens, grad_output, memories, grad_last, norm_gain, query_weight, key_weight, value_weight, out_weight):
    position = lax.axis_index("seg")
    n_seg = lax.axis_size("seg")
    docs = lax.axis_size("dp")
    turns = n_seg // SPAN
    tok, gout, mem, last, gain = tokens[0], grad_output[0], memories[0, 0], grad_last[0], norm_gain[None]

    shard = jnp.concatenate([query_weight, key_weight, value_weight, out_weight.T], axis=1)
    w = lax.all_gather(shard, "dp", axis=0, tiled=True)
    near = runs(n_seg, SPAN, 1)
    mem4 = lax.all_gather(mem, "seg", axis=0, tiled=True, axis_index_groups=near)

    normed, qg, part, kvp, wt = call(
        token_kernel,
        [
            shape((ROWS, D)),
            shape((TOK, D)),
            shape((ROWS, 2 * KV), F32),
            shape((SPAN * ROWS, 2 * KV)),
            shape((D + 2 * KV, D)),
        ],
        (mem, tok, gout, gain, w),
        1_500_000_000,
    )
    kvp4 = spread(kvp, "seg", near)
    mixed, qkv4, hw4, inv4, arrived = call(
        mix_kernel,
        [
            shape((D + 2 * KV, D)),
            shape((SPAN * MEM, D + 2 * KV), F32),
            shape((SPAN * MEM, D), F32),
            shape((SPAN * MEM, 1), F32),
            shape((MEM, D)),
        ],
        (mem4, last, gain, w, wt),
        4_000_000_000,
    )
    count = SPAN * GROUPS
    probs_k, probs_q, krep, vrep, zq = call(
        ready_kernel,
        [
            shape((count, ROWS, PER_GROUP * MEM), F32),
            shape((count, PER_GROUP * MEM, ROWS), F32),
            shape((count, ROWS, WIDE)),
            shape((count, ROWS, WIDE)),
            shape((count, PER_GROUP * MEM, WIDE)),
        ],
        (qkv4, kvp4),
        400_000_000,
    )
    block = position // SPAN
    u4 = kvp4
    for turn in range(turns):
        fresh = (block == turns - 1 - turn).astype(jnp.int32)[None]
        send, u4, grads4 = call(
            functools.partial(chain_kernel, turn > 0),
            [shape((MEM, D)), shape((SPAN * MEM, D)), shape((SPAN * MEM, D + 2 * KV))],
            (fresh, arrived, u4, mixed, probs_k, probs_q, krep, vrep, zq, qkv4, hw4, inv4, kvp4),
            1_000_000_000,
            scalars=1,
        )
        if turn < turns - 1:
            route = [(i, i - SPAN) for i in range((turns - 1 - turn) * SPAN, (turns - turn) * SPAN)]
            arrived = lax.ppermute(send, "seg", route)
    place = jnp.stack([position % SPAN, lax.axis_index("dp") % 2]).astype(jnp.int32)
    half = (docs // 2, D // docs, 2 * KV)
    kv_grad, mine, other = call(
        weight_kernel,
        [shape((ROWS, 2 * KV)), shape(half), shape(half)],
        (place, u4, probs_k, krep, vrep, zq, part, normed),
        400_000_000,
        scalars=1,
    )
    total = reduced(mine, other) / docs
    own, change = call(
        memory_kernel,
        [shape((MEM, D), F32), shape((turns, MEM, D))],
        (place, grads4, wt, mem4, inv4, gain),
        400_000_000,
        scalars=1,
    )
    changes = spread(change, "seg", runs(n_seg, turns, SPAN))
    later = (jnp.arange(turns) > block)[:, None, None]
    after = jnp.sum(jnp.where(later, changes.astype(F32), 0.0), axis=0)
    grad_memories = (last.astype(F32) + after + own).astype(BF)
    (grad_tokens,) = call(rows_kernel, [shape((TOK, D))], (tok, gout, gain, wt, qg, kv_grad), 500_000_000)
    return (grad_tokens[None], grad_memories[None, None], total[:, :KV], total[:, KV:])


def solution(mesh):
    in_specs = (
        P("dp", "seg", None),
        P("dp", "seg", None),
        P("dp", "seg", None, None),
        P("dp", None, None),
        P(),
        P("dp", None),
        P("dp", None),
        P("dp", None),
        P(None, "dp"),
    )
    out_specs = (P("dp", "seg", None), P("dp", "seg", None, None), P("dp", None), P("dp", None))
    return jax.shard_map(body, mesh=mesh, in_specs=in_specs, out_specs=out_specs, check_vma=False)
```

```python
import functools

import jax
import jax.numpy as jnp
from jax import lax
from jax.experimental import pallas as pl
from jax.experimental.pallas import tpu as pltpu
from jax.sharding import PartitionSpec as P

D = 1024
GROUPS = 4
PER_GROUP = 4
HEAD = 64
WIDE = PER_GROUP * HEAD
KV = GROUPS * HEAD
MEM = 32
TOK = 128
ROWS = MEM + TOK
SPAN = 4
EPS = 1e-05
SCALE = 0.125
BF = jnp.bfloat16
F32 = jnp.float32


def nn(a, b):
    return lax.dot_general(a, b, (((1,), (0,)), ((), ())), preferred_element_type=F32)


def nt(a, b):
    return lax.dot_general(a, b, (((1,), (1,)), ((), ())), preferred_element_type=F32)


def tn(a, b):
    return lax.dot_general(a, b, (((0,), (0,)), ((), ())), preferred_element_type=F32)


def normalised(rows, gain):
    inverse = lax.rsqrt(jnp.mean(rows * rows, axis=-1, keepdims=True) + EPS)
    return inverse, (rows * inverse * gain).astype(BF)


def norm_backward(cotangent, normed_grad, hidden, inverse, gain):
    scaled = normed_grad * gain
    mean = jnp.mean(scaled * hidden, axis=-1, keepdims=True)
    return cotangent + inverse * (scaled - hidden * (inverse * inverse * mean))


def repeated(rows, g):
    half = rows[:, (g // 2) * 128 : (g // 2) * 128 + 128].astype(F32)
    lane = lax.broadcasted_iota(jnp.int32, half.shape, 1)
    kept = jnp.where((lane < HEAD) == (g % 2 == 0), half, 0.0)
    both = kept + pltpu.roll(kept, HEAD, 1)
    return jnp.concatenate([both, both], axis=1).astype(BF)


def stacked(rows):
    rows = rows.astype(F32)
    lane = lax.broadcasted_iota(jnp.int32, rows.shape, 1) // HEAD
    return jnp.concatenate([jnp.where(lane == a, rows, 0.0) for a in range(PER_GROUP)], axis=0).astype(BF)


def unstacked(rows):
    n = rows.shape[0] // PER_GROUP
    lane = lax.broadcasted_iota(jnp.int32, (n, WIDE), 1) // HEAD
    total = jnp.zeros((n, WIDE), F32)
    for a in range(PER_GROUP):
        total = jnp.where(lane == a, rows[a * n : (a + 1) * n], total)
    return total


def folded(parts):
    sums = []
    for part in parts:
        half = part[:, :128] + part[:, 128:]
        sums.append(half + pltpu.roll(half, HEAD, 1))
    lane = lax.broadcasted_iota(jnp.int32, sums[0].shape, 1)
    return jnp.concatenate(
        [jnp.where(lane < HEAD, sums[0], sums[1]), jnp.where(lane < HEAD, sums[2], sums[3])], axis=1
    )


def centred(scores_sum_axis, probs, products):
    total = jnp.sum(products, axis=scores_sum_axis, keepdims=True)
    return ((products - probs * total) * SCALE).astype(BF)


def group_columns(g):
    return slice(g * WIDE, (g + 1) * WIDE)


def loads(pairs, sems):
    copies = [pltpu.make_async_copy(src, dst, sems.at[i]) for i, (src, dst) in enumerate(pairs)]
    for copy in copies:
        copy.start()
    return copies


def token_kernel(
    mem_hbm, tok_hbm, gout_hbm, gain_hbm, w_hbm, normed_out, qg_out, part_out, kvp_out, wt_out, w, mem, tok, gout, gain, sems
):
    first, second = slice(0, D + 2 * KV), slice(D + 2 * KV, 2 * D + 2 * KV)
    copies = loads(
        [
            (mem_hbm, mem),
            (tok_hbm, tok),
            (gain_hbm, gain),
            (w_hbm.at[:, first], w.at[:, first]),
            (gout_hbm, gout),
            (w_hbm.at[:, second], w.at[:, second]),
        ],
        sems,
    )
    for copy in copies[:3]:
        copy.wait()
    hidden = jnp.concatenate([mem[...].astype(F32), tok[...].astype(F32)], axis=0)
    _, normed = normalised(hidden, gain[...])
    normed_out[...] = normed
    copies[3].wait()
    q = nn(normed[MEM:], w[:, :D])
    kv = nn(normed, w[:, D : D + 2 * KV]).astype(BF)
    copies[4].wait()
    copies[5].wait()
    up = nn(gout[...], w[:, D + 2 * KV :])
    k, v = kv[:, :KV], kv[:, KV:]
    key_at = lax.broadcasted_iota(jnp.int32, (ROWS, PER_GROUP * TOK), 0)
    row_at = lax.broadcasted_iota(jnp.int32, (ROWS, PER_GROUP * TOK), 1) % TOK
    seen = key_at <= row_at + MEM
    key_parts, value_parts = [], []
    for g in range(GROUPS):
        cols = group_columns(g)
        zq = stacked(q[:, cols])
        zu = stacked(up[:, cols])
        krep, vrep = repeated(k, g), repeated(v, g)
        raised = jnp.where(seen, jnp.exp(nt(krep, zq) * SCALE), 0.0)
        probs = raised * (1.0 / jnp.sum(raised, axis=0, keepdims=True))
        score_grad = centred(0, probs, probs * nt(vrep, zu))
        key_parts.append(nn(score_grad, zq))
        value_parts.append(nn(probs.astype(BF), zu))
        qg_out[:, cols] = unstacked(tn(score_grad, krep)).astype(BF)
    part = jnp.concatenate([folded(key_parts), folded(value_parts)], axis=1)
    part_out[...] = part
    kvp_out[:MEM, :] = part[:MEM].astype(BF)
    kvp_out[MEM:, :] = kv[MEM:]
    wt_out[...] = w[:, : D + 2 * KV].T


def mix_kernel(mem4_hbm, last_hbm, gain_hbm, w, wt, mixed_out, qkv_out, hw_out, inv_out, u_out, mem4, last, gain, sems):
    for copy in loads([(mem4_hbm, mem4), (last_hbm, last), (gain_hbm, gain)], sems):
        copy.wait()
    inverse, normed = normalised(mem4[...].astype(F32), gain[...])
    inv_out[...] = inverse
    hw_out[...] = nn(mem4[...], w[:, D + 2 * KV :])
    qkv_out[...] = nn(normed, w[:, : D + 2 * KV])
    u_out[...] = nn(last[...], w[:, D + 2 * KV :]).astype(BF)
    scaled = (wt[...].astype(F32) * gain[...]).astype(BF)
    mixed_out[...] = nn(scaled, w[:, D + 2 * KV :]).astype(BF)


def ready_kernel(place, qkv4, *refs):
    parts, (probs_k_out, probs_q_out, krep_out, vrep_out, zq_out, near_out) = refs[:SPAN], refs[SPAN:]
    for ahead, kvp in enumerate(parts):
        s = (place[0] + ahead) % SPAN
        rows = pl.ds(pl.multiple_of(s * MEM, MEM), MEM)
        qkv = qkv4[rows, :]
        near_out[rows, :] = kvp[:MEM, :].astype(F32)
        k = jnp.concatenate([qkv[:, D : D + KV].astype(BF), kvp[MEM:, :KV]], axis=0)
        v = jnp.concatenate([qkv[:, D + KV :].astype(BF), kvp[MEM:, KV:]], axis=0)
        zqs = [stacked(qkv[:, group_columns(g)]) for g in range(GROUPS)]
        kreps = [repeated(k, g) for g in range(GROUPS)]
        raised_k = [jnp.exp(nt(krep, zq) * SCALE) for krep, zq in zip(kreps, zqs)]
        raised_q = [jnp.exp(nt(zq, krep) * SCALE) for krep, zq in zip(kreps, zqs)]
        for g in range(GROUPS):
            at = s * GROUPS + g
            probs_k_out[at] = raised_k[g] * (1.0 / jnp.sum(raised_k[g], axis=0, keepdims=True))
            probs_q_out[at] = raised_q[g] * (1.0 / jnp.sum(raised_q[g], axis=1, keepdims=True))
            krep_out[at] = kreps[g]
            vrep_out[at] = repeated(v, g)
            zq_out[at] = zqs[g]


def chain_kernel(
    turn, place, arrived, before, mixed, probs_k, probs_q, krep, vrep, zq, qkv4, hw4, inv4, near, send_out, u_out, grads_out
):
    up = arrived[...].astype(F32)
    if turn > 0:
        up = jnp.where(place[2] == turn, up, before[(SPAN - 1) * MEM :, :].astype(F32))
    for s in reversed(range(SPAN)):
        rows = slice(s * MEM, (s + 1) * MEM)
        u_out[rows, :] = up.astype(BF)
        ats = range(s * GROUPS, (s + 1) * GROUPS)
        zus = [stacked(up[:, group_columns(g)]) for g in range(GROUPS)]
        by_query = [probs_q[at] * nt(zu, vrep[at]) for at, zu in zip(ats, zus)]
        by_key = [probs_k[at] * nt(vrep[at], zu) for at, zu in zip(ats, zus)]
        value_parts = [nn(probs_k[at, :MEM].astype(BF), zu) for at, zu in zip(ats, zus)]
        score_grads = [centred(1, probs_q[at], products) for at, products in zip(ats, by_query)]
        totals = [jnp.sum(products, axis=0, keepdims=True) for products in by_key]
        near_grads = [
            ((products[:MEM] - probs_k[at, :MEM] * total) * SCALE).astype(BF)
            for at, products, total in zip(ats, by_key, totals)
        ]
        query_grads = [unstacked(nn(grad, krep[at])) for at, grad in zip(ats, score_grads)]
        key_parts = [nn(grad, zq[at]) for at, grad in zip(ats, near_grads)]
        kv_grad = jnp.concatenate([folded(key_parts), folded(value_parts)], axis=1) + near[rows, :]
        grads = jnp.concatenate(query_grads + [kv_grad], axis=1).astype(BF)
        grads_out[rows, :] = grads
        inverse = inv4[rows, :]
        along = jnp.sum(grads.astype(F32) * qkv4[rows, :], axis=-1, keepdims=True) * (inverse * inverse / D)
        up = up + inverse * nn(grads, mixed[...]) - along * hw4[rows, :]
    send_out[...] = up.astype(BF)


def weight_kernel(place, u4, probs, krep, vrep, zq, part, normed, kv_out, mine_out, other_out):
    r = place[0]
    up = u4[pl.ds(pl.multiple_of(r * MEM, MEM), MEM), :]
    ats = [r * GROUPS + g for g in range(GROUPS)]
    zus = [stacked(up[:, group_columns(g)]) for g in range(GROUPS)]
    ps = [probs[at] for at in ats]
    products = [p * nt(vrep[at], zu) for at, p, zu in zip(ats, ps, zus)]
    value_parts = [nn(p.astype(BF), zu) for p, zu in zip(ps, zus)]
    score_grads = [centred(0, p, product) for p, product in zip(ps, products)]
    key_parts = [nn(grad, zq[at]) for at, grad in zip(ats, score_grads)]
    kv_grad = jnp.concatenate([folded(key_parts), folded(value_parts)], axis=1) + part[...]
    kv_grad = kv_grad.astype(BF)
    kv_out[...] = kv_grad
    share = mine_out.shape[1]
    grad = tn(normed[...], kv_grad).reshape(mine_out.shape[0], 2, share, 2 * KV)
    first = place[1] == 0
    mine_out[...] = jnp.where(first, grad[:, 0], grad[:, 1]).astype(BF)
    other_out[...] = jnp.where(first, grad[:, 1], grad[:, 0]).astype(BF)


def memory_kernel(place, grads4, wt, mem4, inv4, gain, own_out, all_out):
    hidden, inverse = mem4[...].astype(F32), inv4[...]
    change = norm_backward(0.0, nn(grads4[...], wt[...]), hidden, inverse, gain[...])
    total = jnp.zeros((MEM, D), F32)
    own = jnp.zeros((MEM, D), F32)
    for s in reversed(range(SPAN)):
        total = total + change[s * MEM : (s + 1) * MEM]
        own = jnp.where(place[0] == s, total, own)
    own_out[...] = own
    for copy in range(all_out.shape[0]):
        all_out[copy, :MEM, :] = total[:, : 2 * KV].astype(BF)
        all_out[copy, MEM:, :] = total[:, 2 * KV :].astype(BF)


def rows_kernel(tok, gout, gain, wt, qg, kv_grad, out):
    hidden = tok[...].astype(F32)
    inverse, _ = normalised(hidden, gain[...])
    normed_grad = nn(qg[...], wt[:D, :]) + nn(kv_grad[MEM:, :], wt[D:, :])
    out[...] = norm_backward(gout[...].astype(F32), normed_grad, hidden, inverse, gain[...]).astype(BF)


def call(kernel, outs, args, flops, scalars=0, far=0, scratch=()):
    vmem = pl.BlockSpec(memory_space=pltpu.VMEM)
    smem = pl.BlockSpec(memory_space=pltpu.SMEM)
    hbm = pl.BlockSpec(memory_space=pltpu.HBM)
    args = [
        pltpu.with_memory_space_constraint(a, pltpu.HBM) if scalars <= i < scalars + far else a for i, a in enumerate(args)
    ]
    moved = sum(a.size * a.dtype.itemsize for a in args) + sum(o.size * o.dtype.itemsize for o in outs)
    return pl.pallas_call(
        kernel,
        out_shape=outs,
        in_specs=[smem] * scalars + [hbm] * far + [vmem] * (len(args) - scalars - far),
        out_specs=[vmem] * len(outs),
        scratch_shapes=list(scratch),
        compiler_params=pltpu.CompilerParams(vmem_limit_bytes=20 * 1024 * 1024),
        cost_estimate=pl.CostEstimate(flops=flops, bytes_accessed=moved, transcendentals=0),
    )(*args)


def shape(dims, dtype=BF):
    return jax.ShapeDtypeStruct(dims, dtype)


def runs(axis_size, length, stride):
    block = length * stride
    return [
        [b + o + i * stride for i in range(length)] for b in range(0, axis_size, block) for o in range(stride)
    ]


def spread(block, axis, groups):
    return lax.all_to_all(block, axis, 0, 0, tiled=True, axis_index_groups=groups)


def copies_of(block, count):
    return jnp.broadcast_to(block[None], (count,) + block.shape)


def reduced(mine, other, change):
    docs, n_seg = lax.axis_size("dp"), lax.axis_size("seg")
    turns = n_seg // SPAN
    got = lax.ppermute(other, "dp", [(i, i ^ 1) for i in range(docs)])
    block = (mine.astype(F32) + got.astype(F32)).astype(BF)
    if docs > 2:
        block = lax.all_to_all(block, "dp", 0, 0, tiled=True, axis_index_groups=runs(docs, docs // 2, 2))
    block = jnp.sum(block.astype(F32), axis=0).astype(BF)
    got = spread(copies_of(block, SPAN), "seg", runs(n_seg, SPAN, 1))
    block = jnp.sum(got.astype(F32), axis=0).astype(BF)
    got = spread(jnp.concatenate([copies_of(block, turns), change], axis=1), "seg", runs(n_seg, turns, SPAN))
    rows = block.shape[0]
    changes = jnp.concatenate([got[:, rows : rows + MEM], got[:, rows + MEM :]], axis=2)
    return jnp.sum(got[:, :rows].astype(F32), axis=0), changes


def body(tokens, grad_output, memories, grad_last, norm_gain, query_weight, key_weight, value_weight, out_weight):
    position = lax.axis_index("seg")
    n_seg = lax.axis_size("seg")
    docs = lax.axis_size("dp")
    turns = n_seg // SPAN
    tok, gout, mem, last, gain = tokens[0], grad_output[0], memories[0, 0], grad_last[0], norm_gain[None]
    block = position // SPAN
    place = jnp.stack([position % SPAN, lax.axis_index("dp") % 2, turns - 1 - block]).astype(jnp.int32)

    shard = jnp.concatenate([query_weight, key_weight, value_weight, out_weight.T], axis=1)
    w = lax.all_gather(shard, "dp", axis=0, tiled=True)
    mem4 = lax.all_gather(mem, "seg", axis=0, tiled=True, axis_index_groups=runs(n_seg, SPAN, 1))
    w, mem4, place = lax.optimization_barrier((w, mem4, place))

    dma = pltpu.SemaphoreType.DMA
    normed, qg, part, kvp, wt, w = call(
        token_kernel,
        [
            shape((ROWS, D)),
            shape((TOK, D)),
            shape((ROWS, 2 * KV), F32),
            shape((ROWS, 2 * KV)),
            shape((D + 2 * KV, D)),
            shape((D, 2 * D + 2 * KV)),
        ],
        (mem, tok, gout, gain, w),
        1_500_000_000,
        far=5,
        scratch=(
            pltpu.VMEM((MEM, D), BF),
            pltpu.VMEM((TOK, D), BF),
            pltpu.VMEM((TOK, D), BF),
            pltpu.VMEM((1, D), F32),
            dma((6,)),
        ),
    )
    kvps = [kvp]
    for ahead in range(1, SPAN):
        route = [(i, i // SPAN * SPAN + (i - ahead) % SPAN) for i in range(n_seg)]
        kvps.append(lax.ppermute(kvp, "seg", route))
    mixed, qkv4, hw4, inv4, arrived = call(
        mix_kernel,
        [
            shape((D + 2 * KV, D)),
            shape((SPAN * MEM, D + 2 * KV), F32),
            shape((SPAN * MEM, D), F32),
            shape((SPAN * MEM, 1), F32),
            shape((MEM, D)),
        ],
        (mem4, last, gain, w, wt),
        4_000_000_000,
        far=3,
        scratch=(pltpu.VMEM((SPAN * MEM, D), BF), pltpu.VMEM((MEM, D), BF), pltpu.VMEM((1, D), F32), dma((3,))),
    )
    count = SPAN * GROUPS
    probs_k, probs_q, krep, vrep, zq, near = call(
        ready_kernel,
        [
            shape((count, ROWS, PER_GROUP * MEM), F32),
            shape((count, PER_GROUP * MEM, ROWS), F32),
            shape((count, ROWS, WIDE)),
            shape((count, ROWS, WIDE)),
            shape((count, PER_GROUP * MEM, WIDE)),
            shape((SPAN * MEM, 2 * KV), F32),
        ],
        (place, qkv4, *kvps),
        400_000_000,
        scalars=1,
    )
    u4 = arrived
    for turn in range(turns):
        send, u4, grads4 = call(
            functools.partial(chain_kernel, turn),
            [shape((MEM, D)), shape((SPAN * MEM, D)), shape((SPAN * MEM, D + 2 * KV))],
            (place, arrived, u4, mixed, probs_k, probs_q, krep, vrep, zq, qkv4, hw4, inv4, near),
            1_000_000_000,
            scalars=1,
        )
        if turn < turns - 1:
            route = [(i, i - SPAN) for i in range((turns - 1 - turn) * SPAN, (turns - turn) * SPAN)]
            arrived = lax.ppermute(send, "seg", route)
    half = (docs // 2, D // docs, 2 * KV)
    kv_grad, mine, other = call(
        weight_kernel,
        [shape((ROWS, 2 * KV)), shape(half), shape(half)],
        (place, u4, probs_k, krep, vrep, zq, part, normed),
        400_000_000,
        scalars=1,
    )
    own, change = call(
        memory_kernel,
        [shape((MEM, D), F32), shape((turns, 2 * MEM, 2 * KV))],
        (place, grads4, wt, mem4, inv4, gain),
        400_000_000,
        scalars=1,
    )
    (grad_tokens,) = call(rows_kernel, [shape((TOK, D))], (tok, gout, gain, wt, qg, kv_grad), 500_000_000)
    total, changes = reduced(mine, other, change)
    total = total / docs
    later = (jnp.arange(turns) > block)[:, None, None]
    after = jnp.sum(jnp.where(later, changes.astype(F32), 0.0), axis=0)
    grad_memories = (last.astype(F32) + after + own).astype(BF)
    return (grad_tokens[None], grad_memories[None, None], total[:, :KV], total[:, KV:])


def solution(mesh):
    in_specs = (
        P("dp", "seg", None),
        P("dp", "seg", None),
        P("dp", "seg", None, None),
        P("dp", None, None),
        P(),
        P("dp", None),
        P("dp", None),
        P("dp", None),
        P(None, "dp"),
    )
    out_specs = (P("dp", "seg", None), P("dp", "seg", None, None), P("dp", None), P("dp", None))
    return jax.shard_map(body, mesh=mesh, in_specs=in_specs, out_specs=out_specs, check_vma=False)
```

```python
import functools

import jax
import jax.numpy as jnp
from jax import lax
from jax.experimental import pallas as pl
from jax.experimental.pallas import tpu as pltpu
from jax.sharding import PartitionSpec as P

D = 1024
GROUPS = 4
PER_GROUP = 4
HEAD = 64
WIDE = PER_GROUP * HEAD
KV = GROUPS * HEAD
MEM = 32
TOK = 128
ROWS = MEM + TOK
SPAN = 4
EPS = 1e-05
SCALE = 0.125
BF = jnp.bfloat16
F32 = jnp.float32


def nn(a, b):
    return lax.dot_general(a, b, (((1,), (0,)), ((), ())), preferred_element_type=F32)


def nt(a, b):
    return lax.dot_general(a, b, (((1,), (1,)), ((), ())), preferred_element_type=F32)


def tn(a, b):
    return lax.dot_general(a, b, (((0,), (0,)), ((), ())), preferred_element_type=F32)


def normalised(rows, gain):
    inverse = lax.rsqrt(jnp.mean(rows * rows, axis=-1, keepdims=True) + EPS)
    return inverse, (rows * inverse * gain).astype(BF)


def norm_backward(cotangent, normed_grad, hidden, inverse, gain):
    scaled = normed_grad * gain
    mean = jnp.mean(scaled * hidden, axis=-1, keepdims=True)
    return cotangent + inverse * (scaled - hidden * (inverse * inverse * mean))


def repeated(rows, g):
    half = rows[:, (g // 2) * 128 : (g // 2) * 128 + 128].astype(F32)
    lane = lax.broadcasted_iota(jnp.int32, half.shape, 1)
    kept = jnp.where((lane < HEAD) == (g % 2 == 0), half, 0.0)
    both = kept + pltpu.roll(kept, HEAD, 1)
    return jnp.concatenate([both, both], axis=1).astype(BF)


def stacked(rows):
    rows = rows.astype(F32)
    lane = lax.broadcasted_iota(jnp.int32, rows.shape, 1) // HEAD
    return jnp.concatenate([jnp.where(lane == a, rows, 0.0) for a in range(PER_GROUP)], axis=0).astype(BF)


def unstacked(rows):
    n = rows.shape[0] // PER_GROUP
    lane = lax.broadcasted_iota(jnp.int32, (n, WIDE), 1) // HEAD
    total = jnp.zeros((n, WIDE), F32)
    for a in range(PER_GROUP):
        total = jnp.where(lane == a, rows[a * n : (a + 1) * n], total)
    return total


def folded(parts):
    sums = []
    for part in parts:
        half = part[:, :128] + part[:, 128:]
        sums.append(half + pltpu.roll(half, HEAD, 1))
    lane = lax.broadcasted_iota(jnp.int32, sums[0].shape, 1)
    return jnp.concatenate(
        [jnp.where(lane < HEAD, sums[0], sums[1]), jnp.where(lane < HEAD, sums[2], sums[3])], axis=1
    )


def centred(scores_sum_axis, probs, products):
    total = jnp.sum(products, axis=scores_sum_axis, keepdims=True)
    return ((products - probs * total) * SCALE).astype(BF)


def group_columns(g):
    return slice(g * WIDE, (g + 1) * WIDE)


def loads(pairs, sems):
    copies = [pltpu.make_async_copy(src, dst, sems.at[i]) for i, (src, dst) in enumerate(pairs)]
    for copy in copies:
        copy.start()
    return copies


def token_kernel(
    mem_hbm, tok_hbm, gout_hbm, gain_hbm, w_hbm, normed_out, qg_out, part_out, kvp_out, wt_out, w, mem, tok, gout, gain, sems
):
    first, second = slice(0, D + 2 * KV), slice(D + 2 * KV, 2 * D + 2 * KV)
    copies = loads(
        [
            (mem_hbm, mem),
            (tok_hbm, tok),
            (gain_hbm, gain),
            (w_hbm.at[:, first], w.at[:, first]),
            (gout_hbm, gout),
            (w_hbm.at[:, second], w.at[:, second]),
        ],
        sems,
    )
    for copy in copies[:3]:
        copy.wait()
    hidden = jnp.concatenate([mem[...].astype(F32), tok[...].astype(F32)], axis=0)
    _, normed = normalised(hidden, gain[...])
    normed_out[...] = normed
    copies[3].wait()
    q = nn(normed[MEM:], w[:, :D])
    kv = nn(normed, w[:, D : D + 2 * KV]).astype(BF)
    copies[4].wait()
    copies[5].wait()
    up = nn(gout[...], w[:, D + 2 * KV :])
    k, v = kv[:, :KV], kv[:, KV:]
    key_at = lax.broadcasted_iota(jnp.int32, (ROWS, PER_GROUP * TOK), 0)
    row_at = lax.broadcasted_iota(jnp.int32, (ROWS, PER_GROUP * TOK), 1) % TOK
    seen = key_at <= row_at + MEM
    key_parts, value_parts = [], []
    for g in range(GROUPS):
        cols = group_columns(g)
        zq = stacked(q[:, cols])
        zu = stacked(up[:, cols])
        krep, vrep = repeated(k, g), repeated(v, g)
        raised = jnp.where(seen, jnp.exp(nt(krep, zq) * SCALE), 0.0)
        probs = raised * (1.0 / jnp.sum(raised, axis=0, keepdims=True))
        score_grad = centred(0, probs, probs * nt(vrep, zu))
        key_parts.append(nn(score_grad, zq))
        value_parts.append(nn(probs.astype(BF), zu))
        qg_out[:, cols] = unstacked(tn(score_grad, krep)).astype(BF)
    part = jnp.concatenate([folded(key_parts), folded(value_parts)], axis=1)
    part_out[...] = part
    kvp_out[:MEM, :] = part[:MEM].astype(BF)
    kvp_out[MEM:, :] = kv[MEM:]
    wt_out[...] = w[:, : D + 2 * KV].T


def mix_kernel(mem4_hbm, last_hbm, gain_hbm, w, wt, mixed_out, qkv_out, hw_out, inv_out, u_out, mem4, last, gain, sems):
    for copy in loads([(mem4_hbm, mem4), (last_hbm, last), (gain_hbm, gain)], sems):
        copy.wait()
    inverse, normed = normalised(mem4[...].astype(F32), gain[...])
    inv_out[...] = inverse
    hw_out[...] = nn(mem4[...], w[:, D + 2 * KV :])
    qkv_out[...] = nn(normed, w[:, : D + 2 * KV])
    u_out[...] = nn(last[...], w[:, D + 2 * KV :]).astype(BF)
    scaled = (wt[...].astype(F32) * gain[...]).astype(BF)
    mixed_out[...] = nn(scaled, w[:, D + 2 * KV :]).astype(BF)


def ready_kernel(place, qkv4, *refs):
    parts, (probs_k_out, probs_q_out, krep_out, vrep_out, zq_out, near_out) = refs[:SPAN], refs[SPAN:]
    for ahead, kvp in enumerate(parts):
        s = (place[0] + ahead) % SPAN
        rows = pl.ds(pl.multiple_of(s * MEM, MEM), MEM)
        qkv = qkv4[rows, :]
        near_out[rows, :] = kvp[:MEM, :].astype(F32)
        k = jnp.concatenate([qkv[:, D : D + KV].astype(BF), kvp[MEM:, :KV]], axis=0)
        v = jnp.concatenate([qkv[:, D + KV :].astype(BF), kvp[MEM:, KV:]], axis=0)
        zqs = [stacked(qkv[:, group_columns(g)]) for g in range(GROUPS)]
        kreps = [repeated(k, g) for g in range(GROUPS)]
        raised_k = [jnp.exp(nt(krep, zq) * SCALE) for krep, zq in zip(kreps, zqs)]
        raised_q = [jnp.exp(nt(zq, krep) * SCALE) for krep, zq in zip(kreps, zqs)]
        for g in range(GROUPS):
            at = s * GROUPS + g
            probs_k_out[at] = raised_k[g] * (1.0 / jnp.sum(raised_k[g], axis=0, keepdims=True))
            probs_q_out[at] = raised_q[g] * (1.0 / jnp.sum(raised_q[g], axis=1, keepdims=True))
            krep_out[at] = kreps[g]
            vrep_out[at] = repeated(v, g)
            zq_out[at] = zqs[g]


def chain_kernel(
    turn, place, arrived, before, mixed, probs_k, probs_q, krep, vrep, zq, qkv4, hw4, inv4, near, send_out, u_out, grads_out
):
    up = arrived[...].astype(F32)
    if turn > 0:
        up = jnp.where(place[2] == turn, up, before[(SPAN - 1) * MEM :, :].astype(F32))
    for s in reversed(range(SPAN)):
        rows = slice(s * MEM, (s + 1) * MEM)
        u_out[rows, :] = up.astype(BF)
        ats = range(s * GROUPS, (s + 1) * GROUPS)
        zus = [stacked(up[:, group_columns(g)]) for g in range(GROUPS)]
        by_query = [probs_q[at] * nt(zu, vrep[at]) for at, zu in zip(ats, zus)]
        by_key = [probs_k[at] * nt(vrep[at], zu) for at, zu in zip(ats, zus)]
        value_parts = [nn(probs_k[at, :MEM].astype(BF), zu) for at, zu in zip(ats, zus)]
        score_grads = [centred(1, probs_q[at], products) for at, products in zip(ats, by_query)]
        totals = [jnp.sum(products, axis=0, keepdims=True) for products in by_key]
        near_grads = [
            ((products[:MEM] - probs_k[at, :MEM] * total) * SCALE).astype(BF)
            for at, products, total in zip(ats, by_key, totals)
        ]
        query_grads = [unstacked(nn(grad, krep[at])) for at, grad in zip(ats, score_grads)]
        key_parts = [nn(grad, zq[at]) for at, grad in zip(ats, near_grads)]
        kv_grad = jnp.concatenate([folded(key_parts), folded(value_parts)], axis=1) + near[rows, :]
        grads = jnp.concatenate(query_grads + [kv_grad], axis=1).astype(BF)
        grads_out[rows, :] = grads
        inverse = inv4[rows, :]
        along = jnp.sum(grads.astype(F32) * qkv4[rows, :], axis=-1, keepdims=True) * (inverse * inverse / D)
        up = up + inverse * nn(grads, mixed[...]) - along * hw4[rows, :]
    send_out[...] = up.astype(BF)


def weight_kernel(place, u4, probs, krep, vrep, zq, part, normed, kv_out, mine_out, other_out):
    r = place[0]
    up = u4[pl.ds(pl.multiple_of(r * MEM, MEM), MEM), :]
    ats = [r * GROUPS + g for g in range(GROUPS)]
    zus = [stacked(up[:, group_columns(g)]) for g in range(GROUPS)]
    ps = [probs[at] for at in ats]
    products = [p * nt(vrep[at], zu) for at, p, zu in zip(ats, ps, zus)]
    value_parts = [nn(p.astype(BF), zu) for p, zu in zip(ps, zus)]
    score_grads = [centred(0, p, product) for p, product in zip(ps, products)]
    key_parts = [nn(grad, zq[at]) for at, grad in zip(ats, score_grads)]
    kv_grad = jnp.concatenate([folded(key_parts), folded(value_parts)], axis=1) + part[...]
    kv_grad = kv_grad.astype(BF)
    kv_out[...] = kv_grad
    grad = tn(normed[...], kv_grad)
    grad = grad.reshape(mine_out.shape[0], 2, mine_out.shape[1], 2 * KV)
    first = place[1] == 0
    mine_out[...] = jnp.where(first, grad[:, 0], grad[:, 1]).astype(BF)
    other_out[...] = jnp.where(first, grad[:, 1], grad[:, 0]).astype(BF)


def memory_kernel(turn, place, arrived, held, grads4, wt, mem4, inv4, gain, *outs):
    current = arrived[...].astype(F32)
    if turn > 0:
        current = jnp.where(place[2] == turn, current, held[...].astype(F32))
    hidden, inverse = mem4[...].astype(F32), inv4[...]
    change = norm_backward(0.0, nn(grads4[...], wt[...]), hidden, inverse, gain[...])
    if len(outs) > 1:
        outs[1][...] = current.astype(BF)
        for s in range(SPAN):
            current = current + change[s * MEM : (s + 1) * MEM]
        outs[0][...] = current.astype(BF)
        return
    own = current
    for s in reversed(range(SPAN)):
        current = current + change[s * MEM : (s + 1) * MEM]
        own = jnp.where(place[0] == s, current, own)
    outs[0][...] = own.astype(BF)


def rows_kernel(tok, gout, gain, wt, qg, kv_grad, out):
    hidden = tok[...].astype(F32)
    inverse, _ = normalised(hidden, gain[...])
    normed_grad = nn(qg[...], wt[:D, :]) + nn(kv_grad[MEM:, :], wt[D:, :])
    out[...] = norm_backward(gout[...].astype(F32), normed_grad, hidden, inverse, gain[...]).astype(BF)


def call(kernel, outs, args, flops, scalars=0, far=0, scratch=()):
    vmem = pl.BlockSpec(memory_space=pltpu.VMEM)
    smem = pl.BlockSpec(memory_space=pltpu.SMEM)
    hbm = pl.BlockSpec(memory_space=pltpu.HBM)
    args = [
        pltpu.with_memory_space_constraint(a, pltpu.HBM) if scalars <= i < scalars + far else a for i, a in enumerate(args)
    ]
    moved = sum(a.size * a.dtype.itemsize for a in args) + sum(o.size * o.dtype.itemsize for o in outs)
    return pl.pallas_call(
        kernel,
        out_shape=outs,
        in_specs=[smem] * scalars + [hbm] * far + [vmem] * (len(args) - scalars - far),
        out_specs=[vmem] * len(outs),
        scratch_shapes=list(scratch),
        compiler_params=pltpu.CompilerParams(vmem_limit_bytes=20 * 1024 * 1024),
        cost_estimate=pl.CostEstimate(flops=flops, bytes_accessed=moved, transcendentals=0),
    )(*args)


def shape(dims, dtype=BF):
    return jax.ShapeDtypeStruct(dims, dtype)


def runs(axis_size, length, stride):
    block = length * stride
    return [
        [b + o + i * stride for i in range(length)] for b in range(0, axis_size, block) for o in range(stride)
    ]


def summed_over_documents(mine, other):
    docs = lax.axis_size("dp")
    got = lax.ppermute(other, "dp", [(i, i ^ 1) for i in range(docs)])
    block = (mine.astype(F32) + got.astype(F32)).astype(BF)
    if docs > 2:
        block = lax.all_to_all(block, "dp", 0, 0, tiled=True, axis_index_groups=runs(docs, docs // 2, 2))
    return jnp.sum(block.astype(F32), axis=0).astype(BF)


def summed_over_segments(block):
    n_seg = lax.axis_size("seg")
    copies = jnp.broadcast_to(block[None], (n_seg,) + block.shape)
    return jnp.sum(lax.all_to_all(copies, "seg", 0, 0, tiled=True).astype(F32), axis=0)


def body(tokens, grad_output, memories, grad_last, norm_gain, query_weight, key_weight, value_weight, out_weight):
    position = lax.axis_index("seg")
    n_seg = lax.axis_size("seg")
    docs = lax.axis_size("dp")
    turns = n_seg // SPAN
    tok, gout, mem, last, gain = tokens[0], grad_output[0], memories[0, 0], grad_last[0], norm_gain[None]
    block = position // SPAN
    place = jnp.stack([position % SPAN, lax.axis_index("dp") % 2, turns - 1 - block]).astype(jnp.int32)

    shard = jnp.concatenate([query_weight, key_weight, value_weight, out_weight.T], axis=1)
    w = lax.all_gather(shard, "dp", axis=0, tiled=True)
    mem4 = lax.all_gather(mem, "seg", axis=0, tiled=True, axis_index_groups=runs(n_seg, SPAN, 1))
    w, mem4, place = lax.optimization_barrier((w, mem4, place))

    dma = pltpu.SemaphoreType.DMA
    normed, qg, part, kvp, wt, w = call(
        token_kernel,
        [
            shape((ROWS, D)),
            shape((TOK, D)),
            shape((ROWS, 2 * KV), F32),
            shape((ROWS, 2 * KV)),
            shape((D + 2 * KV, D)),
            shape((D, 2 * D + 2 * KV)),
        ],
        (mem, tok, gout, gain, w),
        1_500_000_000,
        far=5,
        scratch=(
            pltpu.VMEM((MEM, D), BF),
            pltpu.VMEM((TOK, D), BF),
            pltpu.VMEM((TOK, D), BF),
            pltpu.VMEM((1, D), F32),
            dma((6,)),
        ),
    )
    kvps = [kvp]
    for ahead in range(1, SPAN):
        route = [(i, i // SPAN * SPAN + (i - ahead) % SPAN) for i in range(n_seg)]
        kvps.append(lax.ppermute(kvp, "seg", route))
    mixed, qkv4, hw4, inv4, arrived = call(
        mix_kernel,
        [
            shape((D + 2 * KV, D)),
            shape((SPAN * MEM, D + 2 * KV), F32),
            shape((SPAN * MEM, D), F32),
            shape((SPAN * MEM, 1), F32),
            shape((MEM, D)),
        ],
        (mem4, last, gain, w, wt),
        4_000_000_000,
        far=3,
        scratch=(pltpu.VMEM((SPAN * MEM, D), BF), pltpu.VMEM((MEM, D), BF), pltpu.VMEM((1, D), F32), dma((3,))),
    )
    count = SPAN * GROUPS
    probs_k, probs_q, krep, vrep, zq, near = call(
        ready_kernel,
        [
            shape((count, ROWS, PER_GROUP * MEM), F32),
            shape((count, PER_GROUP * MEM, ROWS), F32),
            shape((count, ROWS, WIDE)),
            shape((count, ROWS, WIDE)),
            shape((count, PER_GROUP * MEM, WIDE)),
            shape((SPAN * MEM, 2 * KV), F32),
        ],
        (place, qkv4, *kvps),
        400_000_000,
        scalars=1,
    )
    u4 = arrived
    memory_arrived = memory_held = last
    for turn in range(turns):
        send, u4, grads4 = call(
            functools.partial(chain_kernel, turn),
            [shape((MEM, D)), shape((SPAN * MEM, D)), shape((SPAN * MEM, D + 2 * KV))],
            (place, arrived, u4, mixed, probs_k, probs_q, krep, vrep, zq, qkv4, hw4, inv4, near),
            1_000_000_000,
            scalars=1,
        )
        if turn < turns - 1:
            route = [(i, i - SPAN) for i in range((turns - 1 - turn) * SPAN, (turns - turn) * SPAN)]
            arrived = lax.ppermute(send, "seg", route)
            memory_send, memory_held = call(
                functools.partial(memory_kernel, turn),
                [shape((MEM, D)), shape((MEM, D))],
                (place, memory_arrived, memory_held, grads4, wt, mem4, inv4, gain),
                400_000_000,
                scalars=1,
            )
            arrived, memory_send = lax.optimization_barrier((arrived, memory_send))
            memory_arrived = lax.ppermute(memory_send, "seg", route)
    half = (docs // 2, D // docs, 2 * KV)
    kv_grad, mine, other = call(
        weight_kernel,
        [shape((ROWS, 2 * KV)), shape(half), shape(half)],
        (place, u4, probs_k, krep, vrep, zq, part, normed),
        400_000_000,
        scalars=1,
    )
    (grad_memories,) = call(
        functools.partial(memory_kernel, turns - 1),
        [shape((MEM, D))],
        (place, memory_arrived, memory_held, grads4, wt, mem4, inv4, gain),
        400_000_000,
        scalars=1,
    )
    (grad_tokens,) = call(rows_kernel, [shape((TOK, D))], (tok, gout, gain, wt, qg, kv_grad), 500_000_000)
    block = summed_over_documents(mine, other)
    block, grad_tokens, grad_memories = lax.optimization_barrier((block, grad_tokens, grad_memories))
    total = summed_over_segments(block) / docs
    return (grad_tokens[None], grad_memories[None, None], total[:, :KV], total[:, KV:])


def solution(mesh):
    in_specs = (
        P("dp", "seg", None),
        P("dp", "seg", None),
        P("dp", "seg", None, None),
        P("dp", None, None),
        P(),
        P("dp", None),
        P("dp", None),
        P("dp", None),
        P(None, "dp"),
    )
    out_specs = (P("dp", "seg", None), P("dp", "seg", None, None), P("dp", None), P("dp", None))
    return jax.shard_map(body, mesh=mesh, in_specs=in_specs, out_specs=out_specs, check_vma=False)
```

```python
import functools

import jax
import jax.numpy as jnp
from jax import lax
from jax.experimental import pallas as pl
from jax.experimental.pallas import tpu as pltpu
from jax.sharding import PartitionSpec as P

D = 1024
GROUPS = 4
PER_GROUP = 4
HEAD = 64
WIDE = PER_GROUP * HEAD
KV = GROUPS * HEAD
MEM = 32
TOK = 128
ROWS = MEM + TOK
SPAN = 4
EPS = 1e-05
SCALE = 0.125
BF = jnp.bfloat16
F32 = jnp.float32


def nn(a, b):
    return lax.dot_general(a, b, (((1,), (0,)), ((), ())), preferred_element_type=F32)


def nt(a, b):
    return lax.dot_general(a, b, (((1,), (1,)), ((), ())), preferred_element_type=F32)


def tn(a, b):
    return lax.dot_general(a, b, (((0,), (0,)), ((), ())), preferred_element_type=F32)


def normalised(rows, gain):
    inverse = lax.rsqrt(jnp.mean(rows * rows, axis=-1, keepdims=True) + EPS)
    return inverse, (rows * inverse * gain).astype(BF)


def norm_backward(cotangent, normed_grad, hidden, inverse, gain):
    scaled = normed_grad * gain
    mean = jnp.mean(scaled * hidden, axis=-1, keepdims=True)
    return cotangent + inverse * (scaled - hidden * (inverse * inverse * mean))


def repeated(rows, g):
    half = rows[:, (g // 2) * 128 : (g // 2) * 128 + 128].astype(F32)
    lane = lax.broadcasted_iota(jnp.int32, half.shape, 1)
    kept = jnp.where((lane < HEAD) == (g % 2 == 0), half, 0.0)
    both = kept + pltpu.roll(kept, HEAD, 1)
    return jnp.concatenate([both, both], axis=1).astype(BF)


def stacked(rows):
    rows = rows.astype(F32)
    lane = lax.broadcasted_iota(jnp.int32, rows.shape, 1) // HEAD
    return jnp.concatenate([jnp.where(lane == a, rows, 0.0) for a in range(PER_GROUP)], axis=0).astype(BF)


def unstacked(rows):
    n = rows.shape[0] // PER_GROUP
    lane = lax.broadcasted_iota(jnp.int32, (n, WIDE), 1) // HEAD
    total = jnp.zeros((n, WIDE), F32)
    for a in range(PER_GROUP):
        total = jnp.where(lane == a, rows[a * n : (a + 1) * n], total)
    return total


def folded(parts):
    sums = []
    for part in parts:
        half = part[:, :128] + part[:, 128:]
        sums.append(half + pltpu.roll(half, HEAD, 1))
    lane = lax.broadcasted_iota(jnp.int32, sums[0].shape, 1)
    return jnp.concatenate(
        [jnp.where(lane < HEAD, sums[0], sums[1]), jnp.where(lane < HEAD, sums[2], sums[3])], axis=1
    )


def centred(scores_sum_axis, probs, products):
    total = jnp.sum(products, axis=scores_sum_axis, keepdims=True)
    return ((products - probs * total) * SCALE).astype(BF)


def group_columns(g):
    return slice(g * WIDE, (g + 1) * WIDE)


def loads(pairs, sems):
    copies = [pltpu.make_async_copy(src, dst, sems.at[i]) for i, (src, dst) in enumerate(pairs)]
    for copy in copies:
        copy.start()
    return copies


def token_kernel(
    place, mem_hbm, tok_hbm, gout_hbm, gain_hbm, own_hbm, other_hbm,
    normed_out, qg_out, part_out, kvp_out, wt_out, w, wo, mem, tok, gout, gain, sems
):
    core = place[1]
    across, along, rows, _ = own_hbm.shape
    pieces, later = [], []
    inner, outer = slice(0, D + 2 * KV), slice(D + 2 * KV, 2 * D + 2 * KV)
    for source, side in ((own_hbm, core), (other_hbm, 1 - core)):
        for i in range(across):
            for j in range(along):
                start = pl.multiple_of((j * across + i) * 2 * rows + side * rows, rows)
                pieces.append((source.at[i, j, :, inner], w.at[pl.ds(start, rows), :]))
                later.append((source.at[i, j, :, outer], wo.at[pl.ds(start, rows), :]))
    pairs = [(mem_hbm, mem), (tok_hbm, tok), (gain_hbm, gain)] + pieces + [(gout_hbm, gout)] + later
    copies = loads(pairs, sems)
    for copy in copies[:3]:
        copy.wait()
    hidden = jnp.concatenate([mem[...].astype(F32), tok[...].astype(F32)], axis=0)
    _, normed = normalised(hidden, gain[...])
    normed_out[...] = normed
    for copy in copies[3 : 3 + len(pieces)]:
        copy.wait()
    q = nn(normed[MEM:], w[:, :D])
    kv = nn(normed, w[:, D : D + 2 * KV]).astype(BF)
    for copy in copies[3 + len(pieces) :]:
        copy.wait()
    up = nn(gout[...], wo[...])
    k, v = kv[:, :KV], kv[:, KV:]
    key_at = lax.broadcasted_iota(jnp.int32, (ROWS, PER_GROUP * TOK), 0)
    row_at = lax.broadcasted_iota(jnp.int32, (ROWS, PER_GROUP * TOK), 1) % TOK
    seen = key_at <= row_at + MEM
    key_parts, value_parts = [], []
    for g in range(GROUPS):
        cols = group_columns(g)
        zq = stacked(q[:, cols])
        zu = stacked(up[:, cols])
        krep, vrep = repeated(k, g), repeated(v, g)
        raised = jnp.where(seen, jnp.exp(nt(krep, zq) * SCALE), 0.0)
        probs = raised * (1.0 / jnp.sum(raised, axis=0, keepdims=True))
        score_grad = centred(0, probs, probs * nt(vrep, zu))
        key_parts.append(nn(score_grad, zq))
        value_parts.append(nn(probs.astype(BF), zu))
        qg_out[:, cols] = unstacked(tn(score_grad, krep)).astype(BF)
    part = jnp.concatenate([folded(key_parts), folded(value_parts)], axis=1)
    part_out[...] = part
    kvp_out[:MEM, :] = part[:MEM].astype(BF)
    kvp_out[MEM:ROWS, :] = kv[MEM:]
    kvp_out[ROWS : ROWS + MEM, :] = mem[:, : D // 2]
    kvp_out[ROWS + MEM :, :] = mem[:, D // 2 :]
    wt_out[...] = w[...].T


def mix_kernel(last_hbm, gain_hbm, wo, wt, mixed_out, u_out, last, gain, sems):
    for copy in loads([(last_hbm, last), (gain_hbm, gain)], sems):
        copy.wait()
    u_out[...] = nn(last[...], wo[...]).astype(BF)
    scaled = (wt[...].astype(F32) * gain[...]).astype(BF)
    mixed_out[...] = nn(scaled, wo[...]).astype(BF)


def ready_kernel(place, gain, w, wo, *refs):
    parts, refs = refs[:SPAN], refs[SPAN:]
    probs_k_out, probs_q_out, krep_out, vrep_out, zq_out, near_out, mem_out, qkv_out, hw_out, inv_out = refs
    slots = [(place[0] + ahead) % SPAN for ahead in range(SPAN)]
    spans = [pl.ds(pl.multiple_of(s * MEM, MEM), MEM) for s in slots]
    for rows, kvp in zip(spans, parts):
        mem_out[rows, :] = jnp.concatenate([kvp[ROWS : ROWS + MEM, :], kvp[ROWS + MEM :, :]], axis=1)
        near_out[rows, :] = kvp[:MEM, :].astype(F32)
    inverse, normed = normalised(mem_out[...].astype(F32), gain[...])
    inv_out[...] = inverse
    hw_out[...] = nn(mem_out[...], wo[...])
    qkv_out[...] = nn(normed, w[...])
    for s, rows, kvp in zip(slots, spans, parts):
        qkv = qkv_out[rows, :]
        k = jnp.concatenate([qkv[:, D : D + KV].astype(BF), kvp[MEM:ROWS, :KV]], axis=0)
        v = jnp.concatenate([qkv[:, D + KV :].astype(BF), kvp[MEM:ROWS, KV:]], axis=0)
        zqs = [stacked(qkv[:, group_columns(g)]) for g in range(GROUPS)]
        kreps = [repeated(k, g) for g in range(GROUPS)]
        raised_k = [jnp.exp(nt(krep, zq) * SCALE) for krep, zq in zip(kreps, zqs)]
        raised_q = [jnp.exp(nt(zq, krep) * SCALE) for krep, zq in zip(kreps, zqs)]
        for g in range(GROUPS):
            at = s * GROUPS + g
            probs_k_out[at] = raised_k[g] * (1.0 / jnp.sum(raised_k[g], axis=0, keepdims=True))
            probs_q_out[at] = raised_q[g] * (1.0 / jnp.sum(raised_q[g], axis=1, keepdims=True))
            krep_out[at] = kreps[g]
            vrep_out[at] = repeated(v, g)
            zq_out[at] = zqs[g]


def chain_kernel(
    turn, place, arrived, before, mixed, probs_k, probs_q, krep, vrep, zq, qkv4, hw4, inv4, near, send_out, u_out, grads_out
):
    up = arrived[...].astype(F32)
    if turn > 0:
        up = jnp.where(place[2] == turn, up, before[(SPAN - 1) * MEM :, :].astype(F32))
    for s in reversed(range(SPAN)):
        rows = slice(s * MEM, (s + 1) * MEM)
        u_out[rows, :] = up.astype(BF)
        ats = range(s * GROUPS, (s + 1) * GROUPS)
        zus = [stacked(up[:, group_columns(g)]) for g in range(GROUPS)]
        by_query = [probs_q[at] * nt(zu, vrep[at]) for at, zu in zip(ats, zus)]
        by_key = [probs_k[at] * nt(vrep[at], zu) for at, zu in zip(ats, zus)]
        value_parts = [nn(probs_k[at, :MEM].astype(BF), zu) for at, zu in zip(ats, zus)]
        score_grads = [centred(1, probs_q[at], products) for at, products in zip(ats, by_query)]
        totals = [jnp.sum(products, axis=0, keepdims=True) for products in by_key]
        near_grads = [
            ((products[:MEM] - probs_k[at, :MEM] * total) * SCALE).astype(BF)
            for at, products, total in zip(ats, by_key, totals)
        ]
        query_grads = [unstacked(nn(grad, krep[at])) for at, grad in zip(ats, score_grads)]
        key_parts = [nn(grad, zq[at]) for at, grad in zip(ats, near_grads)]
        kv_grad = jnp.concatenate([folded(key_parts), folded(value_parts)], axis=1) + near[rows, :]
        grads = jnp.concatenate(query_grads + [kv_grad], axis=1).astype(BF)
        grads_out[rows, :] = grads
        inverse = inv4[rows, :]
        along = jnp.sum(grads.astype(F32) * qkv4[rows, :], axis=-1, keepdims=True) * (inverse * inverse / D)
        up = up + inverse * nn(grads, mixed[...]) - along * hw4[rows, :]
    send_out[...] = up.astype(BF)


def weight_kernel(place, u4, probs, krep, vrep, zq, part, normed, kv_out, mine_out, other_out):
    r = place[0]
    up = u4[pl.ds(pl.multiple_of(r * MEM, MEM), MEM), :]
    ats = [r * GROUPS + g for g in range(GROUPS)]
    zus = [stacked(up[:, group_columns(g)]) for g in range(GROUPS)]
    ps = [probs[at] for at in ats]
    products = [p * nt(vrep[at], zu) for at, p, zu in zip(ats, ps, zus)]
    value_parts = [nn(p.astype(BF), zu) for p, zu in zip(ps, zus)]
    score_grads = [centred(0, p, product) for p, product in zip(ps, products)]
    key_parts = [nn(grad, zq[at]) for at, grad in zip(ats, score_grads)]
    kv_grad = jnp.concatenate([folded(key_parts), folded(value_parts)], axis=1) + part[...]
    kv_grad = kv_grad.astype(BF)
    kv_out[...] = kv_grad
    grad = tn(normed[...], kv_grad)
    grad = grad.reshape(mine_out.shape[0], 2, mine_out.shape[1], 2 * KV)
    first = place[1] == 0
    mine_out[...] = jnp.where(first, grad[:, 0], grad[:, 1]).astype(BF)
    other_out[...] = jnp.where(first, grad[:, 1], grad[:, 0]).astype(BF)


def memory_kernel(turn, place, arrived, held, grads4, wt, mem4, inv4, gain, *outs):
    current = arrived[...].astype(F32)
    if turn > 0:
        current = jnp.where(place[2] == turn, current, held[...].astype(F32))
    hidden, inverse = mem4[...].astype(F32), inv4[...]
    change = norm_backward(0.0, nn(grads4[...], wt[...]), hidden, inverse, gain[...])
    if len(outs) > 1:
        outs[1][...] = current.astype(BF)
        for s in range(SPAN):
            current = current + change[s * MEM : (s + 1) * MEM]
        outs[0][...] = current.astype(BF)
        return
    own = current
    for s in reversed(range(SPAN)):
        current = current + change[s * MEM : (s + 1) * MEM]
        own = jnp.where(place[0] == s, current, own)
    outs[0][...] = own.astype(BF)


def rows_kernel(tok, gout, gain, wt, qg, kv_grad, out):
    hidden = tok[...].astype(F32)
    inverse, _ = normalised(hidden, gain[...])
    normed_grad = nn(qg[...], wt[:D, :]) + nn(kv_grad[MEM:, :], wt[D:, :])
    out[...] = norm_backward(gout[...].astype(F32), normed_grad, hidden, inverse, gain[...]).astype(BF)


def call(kernel, outs, args, flops, scalars=0, far=0, scratch=()):
    vmem = pl.BlockSpec(memory_space=pltpu.VMEM)
    smem = pl.BlockSpec(memory_space=pltpu.SMEM)
    hbm = pl.BlockSpec(memory_space=pltpu.HBM)
    args = [
        pltpu.with_memory_space_constraint(a, pltpu.HBM) if scalars <= i < scalars + far else a for i, a in enumerate(args)
    ]
    moved = sum(a.size * a.dtype.itemsize for a in args) + sum(o.size * o.dtype.itemsize for o in outs)
    return pl.pallas_call(
        kernel,
        out_shape=outs,
        in_specs=[smem] * scalars + [hbm] * far + [vmem] * (len(args) - scalars - far),
        out_specs=[vmem] * len(outs),
        scratch_shapes=list(scratch),
        compiler_params=pltpu.CompilerParams(vmem_limit_bytes=20 * 1024 * 1024),
        cost_estimate=pl.CostEstimate(flops=flops, bytes_accessed=moved, transcendentals=0),
    )(*args)


def shape(dims, dtype=BF):
    return jax.ShapeDtypeStruct(dims, dtype)


def runs(axis_size, length, stride):
    block = length * stride
    return [
        [b + o + i * stride for i in range(length)] for b in range(0, axis_size, block) for o in range(stride)
    ]


def gathered(shard):
    docs = lax.axis_size("dp")
    block = lax.all_gather(shard, "dp", axis=0, axis_index_groups=runs(docs, docs // 8, 8))
    copies = jnp.broadcast_to(block[None], (4,) + block.shape)
    own = lax.all_to_all(copies, "dp", 0, 0, tiled=True, axis_index_groups=runs(docs, 4, 2))
    return own, lax.ppermute(own, "dp", [(i, i ^ 1) for i in range(docs)])


def summed_over_documents(mine, other):
    docs = lax.axis_size("dp")
    got = lax.ppermute(other, "dp", [(i, i ^ 1) for i in range(docs)])
    block = (mine.astype(F32) + got.astype(F32)).astype(BF)
    if docs > 2:
        block = lax.all_to_all(block, "dp", 0, 0, tiled=True, axis_index_groups=runs(docs, docs // 2, 2))
    return jnp.sum(block.astype(F32), axis=0).astype(BF)


def summed_over_segments(block):
    n_seg = lax.axis_size("seg")
    copies = jnp.broadcast_to(block[None], (n_seg,) + block.shape)
    return jnp.sum(lax.all_to_all(copies, "seg", 0, 0, tiled=True).astype(F32), axis=0)


def body(tokens, grad_output, memories, grad_last, norm_gain, query_weight, key_weight, value_weight, out_weight):
    position = lax.axis_index("seg")
    n_seg = lax.axis_size("seg")
    docs = lax.axis_size("dp")
    turns = n_seg // SPAN
    tok, gout, mem, last, gain = tokens[0], grad_output[0], memories[0, 0], grad_last[0], norm_gain[None]
    block = position // SPAN
    place = jnp.stack([position % SPAN, lax.axis_index("dp") % 2, turns - 1 - block]).astype(jnp.int32)

    near_w, far_w = gathered(jnp.concatenate([query_weight, key_weight, value_weight, out_weight.T], axis=1))
    near_w, far_w, place = lax.optimization_barrier((near_w, far_w, place))

    dma = pltpu.SemaphoreType.DMA
    normed, qg, part, kvp, wt, w, wo = call(
        token_kernel,
        [
            shape((ROWS, D)),
            shape((TOK, D)),
            shape((ROWS, 2 * KV), F32),
            shape((ROWS + 2 * MEM, 2 * KV)),
            shape((D + 2 * KV, D)),
            shape((D, D + 2 * KV)),
            shape((D, D)),
        ],
        (place, mem, tok, gout, gain, near_w, far_w),
        1_500_000_000,
        scalars=1,
        far=6,
        scratch=(
            pltpu.VMEM((MEM, D), BF),
            pltpu.VMEM((TOK, D), BF),
            pltpu.VMEM((TOK, D), BF),
            pltpu.VMEM((1, D), F32),
            dma((4 + 2 * docs,)),
        ),
    )
    kvps = [kvp]
    for ahead in range(1, SPAN):
        route = [(i, i // SPAN * SPAN + (i - ahead) % SPAN) for i in range(n_seg)]
        kvps.append(lax.ppermute(kvp, "seg", route))
    mixed, arrived = call(
        mix_kernel,
        [shape((D + 2 * KV, D)), shape((MEM, D))],
        (last, gain, wo, wt),
        4_000_000_000,
        far=2,
        scratch=(pltpu.VMEM((MEM, D), BF), pltpu.VMEM((1, D), F32), dma((2,))),
    )
    count = SPAN * GROUPS
    probs_k, probs_q, krep, vrep, zq, near, mem4, qkv4, hw4, inv4 = call(
        ready_kernel,
        [
            shape((count, ROWS, PER_GROUP * MEM), F32),
            shape((count, PER_GROUP * MEM, ROWS), F32),
            shape((count, ROWS, WIDE)),
            shape((count, ROWS, WIDE)),
            shape((count, PER_GROUP * MEM, WIDE)),
            shape((SPAN * MEM, 2 * KV), F32),
            shape((SPAN * MEM, D)),
            shape((SPAN * MEM, D + 2 * KV), F32),
            shape((SPAN * MEM, D), F32),
            shape((SPAN * MEM, 1), F32),
        ],
        (place, gain, w, wo, *kvps),
        400_000_000,
        scalars=1,
    )
    u4 = arrived
    memory_arrived = memory_held = last
    for turn in range(turns):
        send, u4, grads4 = call(
            functools.partial(chain_kernel, turn),
            [shape((MEM, D)), shape((SPAN * MEM, D)), shape((SPAN * MEM, D + 2 * KV))],
            (place, arrived, u4, mixed, probs_k, probs_q, krep, vrep, zq, qkv4, hw4, inv4, near),
            1_000_000_000,
            scalars=1,
        )
        if turn < turns - 1:
            route = [(i, i - SPAN) for i in range((turns - 1 - turn) * SPAN, (turns - turn) * SPAN)]
            arrived = lax.ppermute(send, "seg", route)
            memory_send, memory_held = call(
                functools.partial(memory_kernel, turn),
                [shape((MEM, D)), shape((MEM, D))],
                (place, memory_arrived, memory_held, grads4, wt, mem4, inv4, gain),
                400_000_000,
                scalars=1,
            )
            arrived, memory_send = lax.optimization_barrier((arrived, memory_send))
            memory_arrived = lax.ppermute(memory_send, "seg", route)
    half = (docs // 2, D // docs, 2 * KV)
    kv_grad, mine, other = call(
        weight_kernel,
        [shape((ROWS, 2 * KV)), shape(half), shape(half)],
        (place, u4, probs_k, krep, vrep, zq, part, normed),
        400_000_000,
        scalars=1,
    )
    (grad_memories,) = call(
        functools.partial(memory_kernel, turns - 1),
        [shape((MEM, D))],
        (place, memory_arrived, memory_held, grads4, wt, mem4, inv4, gain),
        400_000_000,
        scalars=1,
    )
    (grad_tokens,) = call(rows_kernel, [shape((TOK, D))], (tok, gout, gain, wt, qg, kv_grad), 500_000_000)
    block = summed_over_documents(mine, other)
    block, grad_tokens, grad_memories = lax.optimization_barrier((block, grad_tokens, grad_memories))
    total = summed_over_segments(block) / docs
    return (grad_tokens[None], grad_memories[None, None], total[:, :KV], total[:, KV:])


def solution(mesh):
    in_specs = (
        P("dp", "seg", None),
        P("dp", "seg", None),
        P("dp", "seg", None, None),
        P("dp", None, None),
        P(),
        P("dp", None),
        P("dp", None),
        P("dp", None),
        P(None, "dp"),
    )
    out_specs = (P("dp", "seg", None), P("dp", "seg", None, None), P("dp", None), P("dp", None))
    return jax.shard_map(body, mesh=mesh, in_specs=in_specs, out_specs=out_specs, check_vma=False)
```

```python
import functools

import jax
import jax.numpy as jnp
from jax import lax
from jax.experimental import pallas as pl
from jax.experimental.pallas import tpu as pltpu
from jax.sharding import PartitionSpec as P

D = 1024
GROUPS = 4
PER_GROUP = 4
HEAD = 64
WIDE = PER_GROUP * HEAD
KV = GROUPS * HEAD
MEM = 32
TOK = 128
ROWS = MEM + TOK
SPAN = 4
EPS = 1e-05
SCALE = 0.125
BF = jnp.bfloat16
F32 = jnp.float32


def nn(a, b):
    return lax.dot_general(a, b, (((1,), (0,)), ((), ())), preferred_element_type=F32)


def nt(a, b):
    return lax.dot_general(a, b, (((1,), (1,)), ((), ())), preferred_element_type=F32)


def tn(a, b):
    return lax.dot_general(a, b, (((0,), (0,)), ((), ())), preferred_element_type=F32)


def normalised(rows, gain):
    inverse = lax.rsqrt(jnp.mean(rows * rows, axis=-1, keepdims=True) + EPS)
    return inverse, (rows * inverse * gain).astype(BF)


def norm_backward(cotangent, normed_grad, hidden, inverse, gain):
    scaled = normed_grad * gain
    mean = jnp.mean(scaled * hidden, axis=-1, keepdims=True)
    return cotangent + inverse * (scaled - hidden * (inverse * inverse * mean))


def repeated(rows, g):
    half = rows[:, (g // 2) * 128 : (g // 2) * 128 + 128].astype(F32)
    lane = lax.broadcasted_iota(jnp.int32, half.shape, 1)
    kept = jnp.where((lane < HEAD) == (g % 2 == 0), half, 0.0)
    both = kept + pltpu.roll(kept, HEAD, 1)
    return jnp.concatenate([both, both], axis=1).astype(BF)


def stacked(rows):
    rows = rows.astype(F32)
    lane = lax.broadcasted_iota(jnp.int32, rows.shape, 1) // HEAD
    return jnp.concatenate([jnp.where(lane == a, rows, 0.0) for a in range(PER_GROUP)], axis=0).astype(BF)


def unstacked(rows):
    n = rows.shape[0] // PER_GROUP
    lane = lax.broadcasted_iota(jnp.int32, (n, WIDE), 1) // HEAD
    total = jnp.zeros((n, WIDE), F32)
    for a in range(PER_GROUP):
        total = jnp.where(lane == a, rows[a * n : (a + 1) * n], total)
    return total


def folded(parts):
    sums = []
    for part in parts:
        half = part[:, :128] + part[:, 128:]
        sums.append(half + pltpu.roll(half, HEAD, 1))
    lane = lax.broadcasted_iota(jnp.int32, sums[0].shape, 1)
    return jnp.concatenate(
        [jnp.where(lane < HEAD, sums[0], sums[1]), jnp.where(lane < HEAD, sums[2], sums[3])], axis=1
    )


def centred(scores_sum_axis, probs, products):
    total = jnp.sum(products, axis=scores_sum_axis, keepdims=True)
    return ((products - probs * total) * SCALE).astype(BF)


def group_columns(g):
    return slice(g * WIDE, (g + 1) * WIDE)


def loads(pairs, sems):
    copies = [pltpu.make_async_copy(src, dst, sems.at[i]) for i, (src, dst) in enumerate(pairs)]
    for copy in copies:
        copy.start()
    return copies


def token_kernel(
    place, mem_hbm, tok_hbm, gout_hbm, gain_hbm, own_hbm, other_hbm,
    normed_out, qg_out, part_out, kvp_out, w_out, wo_out, mem, tok, gout, gain, sems
):
    core = place[1]
    near = [(mem_hbm, mem), (tok_hbm, tok), (gain_hbm, gain)]
    first, second = [], []
    inner, outer = slice(0, D + 2 * KV), slice(D + 2 * KV, 2 * D + 2 * KV)
    for i in range(own_hbm.shape[0]):
        for source, side in ((own_hbm, core), (other_hbm, 1 - core)):
            first.append((source.at[i, :, :, inner], w_out.at[:, i, side]))
            second.append((source.at[i, :, :, outer], wo_out.at[:, i, side]))
    copies = loads(near + first + [(gout_hbm, gout)] + second, sems)
    for copy in copies[:3]:
        copy.wait()
    hidden = jnp.concatenate([mem[...].astype(F32), tok[...].astype(F32)], axis=0)
    _, normed = normalised(hidden, gain[...])
    normed_out[...] = normed
    for copy in copies[3 : 3 + len(first)]:
        copy.wait()
    w = w_out[...].reshape(D, D + 2 * KV)
    q = nn(normed[MEM:], w[:, :D])
    kv = nn(normed, w[:, D:]).astype(BF)
    for copy in copies[3 + len(first) :]:
        copy.wait()
    up = nn(gout[...], wo_out[...].reshape(D, D))
    k, v = kv[:, :KV], kv[:, KV:]
    key_at = lax.broadcasted_iota(jnp.int32, (ROWS, PER_GROUP * TOK), 0)
    row_at = lax.broadcasted_iota(jnp.int32, (ROWS, PER_GROUP * TOK), 1) % TOK
    seen = key_at <= row_at + MEM
    key_parts, value_parts = [], []
    for pair in ((0, 1), (2, 3)):
        zqs = [stacked(q[:, group_columns(g)]) for g in pair]
        zus = [stacked(up[:, group_columns(g)]) for g in pair]
        kreps, vreps = [repeated(k, g) for g in pair], [repeated(v, g) for g in pair]
        raised = [jnp.where(seen, jnp.exp(nt(krep, zq) * SCALE), 0.0) for krep, zq in zip(kreps, zqs)]
        products = [nt(vrep, zu) for vrep, zu in zip(vreps, zus)]
        probs = [r * (1.0 / jnp.sum(r, axis=0, keepdims=True)) for r in raised]
        score_grads = [centred(0, p, p * product) for p, product in zip(probs, products)]
        value_parts += [nn(p.astype(BF), zu) for p, zu in zip(probs, zus)]
        key_parts += [nn(grad, zq) for grad, zq in zip(score_grads, zqs)]
        for g, grad, krep in zip(pair, score_grads, kreps):
            qg_out[:, group_columns(g)] = unstacked(tn(grad, krep)).astype(BF)
    part = jnp.concatenate([folded(key_parts), folded(value_parts)], axis=1)
    part_out[...] = part
    kvp_out[:MEM, :] = part[:MEM].astype(BF)
    kvp_out[MEM:ROWS, :] = kv[MEM:]
    kvp_out[ROWS : ROWS + MEM, :] = mem[:, : D // 2]
    kvp_out[ROWS + MEM :, :] = mem[:, D // 2 :]


def mix_kernel(last_hbm, gain_hbm, w, wo, wt, mixed_out, u_out, last, gain, sems):
    for copy in loads([(last_hbm, last), (gain_hbm, gain)], sems):
        copy.wait()
    u_out[...] = nn(last[...], wo[...]).astype(BF)
    wt[...] = w[...].T
    scaled = (wt[...].astype(F32) * gain[...]).astype(BF)
    mixed_out[...] = nn(scaled, wo[...]).astype(BF)


def ready_kernel(place, gain, w, wo, *refs):
    parts, refs = refs[:SPAN], refs[SPAN:]
    probs_k_out, probs_q_out, krep_out, vrep_out, zq_out, near_out, mem_out, qkv_out, hw_out, inv_out = refs
    slots = [(place[0] + ahead) % SPAN for ahead in range(SPAN)]
    spans = [pl.ds(pl.multiple_of(s * MEM, MEM), MEM) for s in slots]
    for rows, kvp in zip(spans, parts):
        mem_out[rows, :] = jnp.concatenate([kvp[ROWS : ROWS + MEM, :], kvp[ROWS + MEM :, :]], axis=1)
        near_out[rows, :] = kvp[:MEM, :].astype(F32)
    inverse, normed = normalised(mem_out[...].astype(F32), gain[...])
    inv_out[...] = inverse
    hw_out[...] = nn(mem_out[...], wo[...])
    qkv_out[...] = nn(normed, w[...])
    for s, rows, kvp in zip(slots, spans, parts):
        qkv = qkv_out[rows, :]
        k = jnp.concatenate([qkv[:, D : D + KV].astype(BF), kvp[MEM:ROWS, :KV]], axis=0)
        v = jnp.concatenate([qkv[:, D + KV :].astype(BF), kvp[MEM:ROWS, KV:]], axis=0)
        zqs = [stacked(qkv[:, group_columns(g)]) for g in range(GROUPS)]
        kreps = [repeated(k, g) for g in range(GROUPS)]
        raised_k = [jnp.exp(nt(krep, zq) * SCALE) for krep, zq in zip(kreps, zqs)]
        raised_q = [jnp.exp(nt(zq, krep) * SCALE) for krep, zq in zip(kreps, zqs)]
        for g in range(GROUPS):
            at = s * GROUPS + g
            probs_k_out[at] = raised_k[g] * (1.0 / jnp.sum(raised_k[g], axis=0, keepdims=True))
            probs_q_out[at] = raised_q[g] * (1.0 / jnp.sum(raised_q[g], axis=1, keepdims=True))
            krep_out[at] = kreps[g]
            vrep_out[at] = repeated(v, g)
            zq_out[at] = zqs[g]


def chain_kernel(
    turn, place, arrived, before, mixed, probs_k, probs_q, krep, vrep, zq, qkv4, hw4, inv4, near, send_out, u_out, grads_out
):
    up = arrived[...].astype(F32)
    if turn > 0:
        up = jnp.where(place[2] == turn, up, before[(SPAN - 1) * MEM :, :].astype(F32))
    for s in reversed(range(SPAN)):
        rows = slice(s * MEM, (s + 1) * MEM)
        u_out[rows, :] = up.astype(BF)
        ats = range(s * GROUPS, (s + 1) * GROUPS)
        zus = [stacked(up[:, group_columns(g)]) for g in range(GROUPS)]
        by_query = [probs_q[at] * nt(zu, vrep[at]) for at, zu in zip(ats, zus)]
        by_key = [probs_k[at] * nt(vrep[at], zu) for at, zu in zip(ats, zus)]
        value_parts = [nn(probs_k[at, :MEM].astype(BF), zu) for at, zu in zip(ats, zus)]
        score_grads = [centred(1, probs_q[at], products) for at, products in zip(ats, by_query)]
        totals = [jnp.sum(products, axis=0, keepdims=True) for products in by_key]
        near_grads = [
            ((products[:MEM] - probs_k[at, :MEM] * total) * SCALE).astype(BF)
            for at, products, total in zip(ats, by_key, totals)
        ]
        query_grads = [unstacked(nn(grad, krep[at])) for at, grad in zip(ats, score_grads)]
        key_parts = [nn(grad, zq[at]) for at, grad in zip(ats, near_grads)]
        kv_grad = jnp.concatenate([folded(key_parts), folded(value_parts)], axis=1) + near[rows, :]
        grads = jnp.concatenate(query_grads + [kv_grad], axis=1).astype(BF)
        grads_out[rows, :] = grads
        inverse = inv4[rows, :]
        along = jnp.sum(grads.astype(F32) * qkv4[rows, :], axis=-1, keepdims=True) * (inverse * inverse / D)
        up = up + inverse * nn(grads, mixed[...]) - along * hw4[rows, :]
    send_out[...] = up.astype(BF)


def weight_kernel(place, u4, probs, krep, vrep, zq, part, normed, kv_out, mine_out, other_out):
    r = place[0]
    up = u4[pl.ds(pl.multiple_of(r * MEM, MEM), MEM), :]
    ats = [r * GROUPS + g for g in range(GROUPS)]
    zus = [stacked(up[:, group_columns(g)]) for g in range(GROUPS)]
    ps = [probs[at] for at in ats]
    products = [p * nt(vrep[at], zu) for at, p, zu in zip(ats, ps, zus)]
    value_parts = [nn(p.astype(BF), zu) for p, zu in zip(ps, zus)]
    score_grads = [centred(0, p, product) for p, product in zip(ps, products)]
    key_parts = [nn(grad, zq[at]) for at, grad in zip(ats, score_grads)]
    kv_grad = jnp.concatenate([folded(key_parts), folded(value_parts)], axis=1) + part[...]
    kv_grad = kv_grad.astype(BF)
    kv_out[...] = kv_grad
    grad = tn(normed[...], kv_grad)
    pieces, depth, _ = mine_out.shape
    share = 8 * pieces
    first = place[1] == 0
    for piece in range(pieces):
        halves = [
            jnp.concatenate([grad[at : at + 8] for at in range(core * share + piece * 8, D, 2 * share)], axis=0)
            for core in range(2)
        ]
        mine_out[piece] = jnp.where(first, halves[0], halves[1]).astype(BF)
        other_out[piece] = jnp.where(first, halves[1], halves[0]).astype(BF)


def memory_kernel(turn, place, arrived, held, grads4, wt, mem4, inv4, gain, *outs):
    current = arrived[...].astype(F32)
    if turn > 0:
        current = jnp.where(place[2] == turn, current, held[...].astype(F32))
    hidden, inverse = mem4[...].astype(F32), inv4[...]
    change = norm_backward(0.0, nn(grads4[...], wt[...]), hidden, inverse, gain[...])
    if len(outs) > 1:
        outs[1][...] = current.astype(BF)
        for s in range(SPAN):
            current = current + change[s * MEM : (s + 1) * MEM]
        outs[0][...] = current.astype(BF)
        return
    own = current
    for s in reversed(range(SPAN)):
        current = current + change[s * MEM : (s + 1) * MEM]
        own = jnp.where(place[0] == s, current, own)
    outs[0][...] = own.astype(BF)


def rows_kernel(tok, gout, gain, wt, qg, kv_grad, out):
    hidden = tok[...].astype(F32)
    inverse, _ = normalised(hidden, gain[...])
    normed_grad = nn(qg[...], wt[:D, :]) + nn(kv_grad[MEM:, :], wt[D:, :])
    out[...] = norm_backward(gout[...].astype(F32), normed_grad, hidden, inverse, gain[...]).astype(BF)


def call(kernel, outs, args, flops, scalars=0, far=0, scratch=()):
    vmem = pl.BlockSpec(memory_space=pltpu.VMEM)
    smem = pl.BlockSpec(memory_space=pltpu.SMEM)
    hbm = pl.BlockSpec(memory_space=pltpu.HBM)
    args = [
        pltpu.with_memory_space_constraint(a, pltpu.HBM) if scalars <= i < scalars + far else a for i, a in enumerate(args)
    ]
    moved = sum(a.size * a.dtype.itemsize for a in args) + sum(o.size * o.dtype.itemsize for o in outs)
    return pl.pallas_call(
        kernel,
        out_shape=outs,
        in_specs=[smem] * scalars + [hbm] * far + [vmem] * (len(args) - scalars - far),
        out_specs=[vmem] * len(outs),
        scratch_shapes=list(scratch),
        compiler_params=pltpu.CompilerParams(vmem_limit_bytes=20 * 1024 * 1024),
        cost_estimate=pl.CostEstimate(flops=flops, bytes_accessed=moved, transcendentals=0),
    )(*args)


def shape(dims, dtype=BF):
    return jax.ShapeDtypeStruct(dims, dtype)


def runs(axis_size, length, stride):
    block = length * stride
    return [
        [b + o + i * stride for i in range(length)] for b in range(0, axis_size, block) for o in range(stride)
    ]


def gathered(shard):
    docs = lax.axis_size("dp")
    block = lax.all_gather(shard, "dp", axis=0, axis_index_groups=runs(docs, docs // 8, 8))
    copies = jnp.broadcast_to(block[None], (4,) + block.shape)
    own = lax.all_to_all(copies, "dp", 0, 0, tiled=True, axis_index_groups=runs(docs, 4, 2))
    return own, lax.ppermute(own, "dp", [(i, i ^ 1) for i in range(docs)])


def summed_over_group(mine, other):
    docs = lax.axis_size("dp")
    got = lax.ppermute(other, "dp", [(i, i ^ 1) for i in range(docs)])
    block = (mine.astype(F32) + got.astype(F32)).astype(BF)
    block = lax.all_to_all(block, "seg", 0, 0, tiled=True, axis_index_groups=runs(lax.axis_size("seg"), SPAN, 1))
    return jnp.sum(block.astype(F32), axis=0).astype(BF)


def summed_over_documents(block):
    docs = lax.axis_size("dp")
    chunks = docs // 2
    block = block.reshape(chunks, 8, 2 * KV)
    block = lax.all_to_all(block, "dp", 0, 0, tiled=True, axis_index_groups=runs(docs, chunks, 2))
    return jnp.sum(block.astype(F32), axis=0).astype(BF)


def summed_over_segments(block):
    n_seg = lax.axis_size("seg")
    copies = jnp.broadcast_to(block[None], (n_seg,) + block.shape)
    got = lax.all_to_all(copies, "seg", 0, 0, tiled=True).reshape(n_seg // SPAN, SPAN, 8, 2 * KV)
    return jnp.sum(got.astype(F32), axis=0).reshape(SPAN * 8, 2 * KV)


def body(tokens, grad_output, memories, grad_last, norm_gain, query_weight, key_weight, value_weight, out_weight):
    position = lax.axis_index("seg")
    n_seg = lax.axis_size("seg")
    docs = lax.axis_size("dp")
    turns = n_seg // SPAN
    tok, gout, mem, last, gain = tokens[0], grad_output[0], memories[0, 0], grad_last[0], norm_gain[None]
    block = position // SPAN
    place = jnp.stack([position % SPAN, lax.axis_index("dp") % 2, turns - 1 - block]).astype(jnp.int32)

    weights = gathered(jnp.concatenate([query_weight, key_weight, value_weight, out_weight.T], axis=1))
    *weights, place = lax.optimization_barrier((*weights, place))

    dma = pltpu.SemaphoreType.DMA
    normed, qg, part, kvp, w, wo = call(
        token_kernel,
        [
            shape((ROWS, D)),
            shape((TOK, D)),
            shape((ROWS, 2 * KV), F32),
            shape((ROWS + 2 * MEM, 2 * KV)),
            shape((docs // 8, 4, 2, D // docs, D + 2 * KV)),
            shape((docs // 8, 4, 2, D // docs, D)),
        ],
        (place, mem, tok, gout, gain, *weights),
        1_500_000_000,
        scalars=1,
        far=6,
        scratch=(
            pltpu.VMEM((MEM, D), BF),
            pltpu.VMEM((TOK, D), BF),
            pltpu.VMEM((TOK, D), BF),
            pltpu.VMEM((1, D), F32),
            dma((4 + 16,)),
        ),
    )
    w, wo = w.reshape(D, D + 2 * KV), wo.reshape(D, D)
    kvps = [kvp]
    for ahead in range(1, SPAN):
        route = [(i, i // SPAN * SPAN + (i - ahead) % SPAN) for i in range(n_seg)]
        kvps.append(lax.ppermute(kvp, "seg", route))
    wt, mixed, arrived = call(
        mix_kernel,
        [shape((D + 2 * KV, D)), shape((D + 2 * KV, D)), shape((MEM, D))],
        (last, gain, w, wo),
        4_000_000_000,
        far=2,
        scratch=(pltpu.VMEM((MEM, D), BF), pltpu.VMEM((1, D), F32), dma((2,))),
    )
    count = SPAN * GROUPS
    probs_k, probs_q, krep, vrep, zq, near, mem4, qkv4, hw4, inv4 = call(
        ready_kernel,
        [
            shape((count, ROWS, PER_GROUP * MEM), F32),
            shape((count, PER_GROUP * MEM, ROWS), F32),
            shape((count, ROWS, WIDE)),
            shape((count, ROWS, WIDE)),
            shape((count, PER_GROUP * MEM, WIDE)),
            shape((SPAN * MEM, 2 * KV), F32),
            shape((SPAN * MEM, D)),
            shape((SPAN * MEM, D + 2 * KV), F32),
            shape((SPAN * MEM, D), F32),
            shape((SPAN * MEM, 1), F32),
        ],
        (place, gain, w, wo, *kvps),
        400_000_000,
        scalars=1,
    )
    u4 = arrived
    memory_arrived = memory_held = last
    for turn in range(turns):
        send, u4, grads4 = call(
            functools.partial(chain_kernel, turn),
            [shape((MEM, D)), shape((SPAN * MEM, D)), shape((SPAN * MEM, D + 2 * KV))],
            (place, arrived, u4, mixed, probs_k, probs_q, krep, vrep, zq, qkv4, hw4, inv4, near),
            1_000_000_000,
            scalars=1,
        )
        if turn < turns - 1:
            route = [(i, i - SPAN) for i in range((turns - 1 - turn) * SPAN, (turns - turn) * SPAN)]
            arrived = lax.ppermute(send, "seg", route)
            memory_send, memory_held = call(
                functools.partial(memory_kernel, turn),
                [shape((MEM, D)), shape((MEM, D))],
                (place, memory_arrived, memory_held, grads4, wt, mem4, inv4, gain),
                400_000_000,
                scalars=1,
            )
            arrived, memory_send = lax.optimization_barrier((arrived, memory_send))
            memory_arrived = lax.ppermute(memory_send, "seg", route)
    half = (SPAN, docs // 2 * 8, 2 * KV)
    kv_grad, mine, other = call(
        weight_kernel,
        [shape((ROWS, 2 * KV)), shape(half), shape(half)],
        (place, u4, probs_k, krep, vrep, zq, part, normed),
        400_000_000,
        scalars=1,
    )
    (grad_memories,) = call(
        functools.partial(memory_kernel, turns - 1),
        [shape((MEM, D))],
        (place, memory_arrived, memory_held, grads4, wt, mem4, inv4, gain),
        400_000_000,
        scalars=1,
    )
    (grad_tokens,) = call(rows_kernel, [shape((TOK, D))], (tok, gout, gain, wt, qg, kv_grad), 500_000_000)
    block = summed_over_group(mine, other)
    block = summed_over_documents(block)
    block, grad_tokens, grad_memories = lax.optimization_barrier((block, grad_tokens, grad_memories))
    total = summed_over_segments(block) / docs
    return (grad_tokens[None], grad_memories[None, None], total[:, :KV], total[:, KV:])


def solution(mesh):
    in_specs = (
        P("dp", "seg", None),
        P("dp", "seg", None),
        P("dp", "seg", None, None),
        P("dp", None, None),
        P(),
        P("dp", None),
        P("dp", None),
        P("dp", None),
        P(None, "dp"),
    )
    out_specs = (P("dp", "seg", None), P("dp", "seg", None, None), P("dp", None), P("dp", None))
    return jax.shard_map(body, mesh=mesh, in_specs=in_specs, out_specs=out_specs, check_vma=False)
```

```python
import functools

import jax
import jax.numpy as jnp
from jax import lax
from jax.experimental import pallas as pl
from jax.experimental.pallas import tpu as pltpu
from jax.sharding import PartitionSpec as P

D = 1024
GROUPS = 4
PER_GROUP = 4
HEAD = 64
WIDE = PER_GROUP * HEAD
KV = GROUPS * HEAD
MEM = 32
TOK = 128
ROWS = MEM + TOK
SPAN = 4
EPS = 1e-05
SCALE = 0.125
BF = jnp.bfloat16
F32 = jnp.float32


def nn(a, b):
    return lax.dot_general(a, b, (((1,), (0,)), ((), ())), preferred_element_type=F32)


def nt(a, b):
    return lax.dot_general(a, b, (((1,), (1,)), ((), ())), preferred_element_type=F32)


def tn(a, b):
    return lax.dot_general(a, b, (((0,), (0,)), ((), ())), preferred_element_type=F32)


def normalised(rows, gain):
    inverse = lax.rsqrt(jnp.mean(rows * rows, axis=-1, keepdims=True) + EPS)
    return inverse, (rows * inverse * gain).astype(BF)


def norm_backward(cotangent, normed_grad, hidden, inverse, gain):
    scaled = normed_grad * gain
    mean = jnp.mean(scaled * hidden, axis=-1, keepdims=True)
    return cotangent + inverse * (scaled - hidden * (inverse * inverse * mean))


def repeated(rows, g):
    half = rows[:, (g // 2) * 128 : (g // 2) * 128 + 128].astype(F32)
    lane = lax.broadcasted_iota(jnp.int32, half.shape, 1)
    kept = jnp.where((lane < HEAD) == (g % 2 == 0), half, 0.0)
    both = kept + pltpu.roll(kept, HEAD, 1)
    return jnp.concatenate([both, both], axis=1).astype(BF)


def stacked(rows):
    rows = rows.astype(F32)
    lane = lax.broadcasted_iota(jnp.int32, rows.shape, 1) // HEAD
    return jnp.concatenate([jnp.where(lane == a, rows, 0.0) for a in range(PER_GROUP)], axis=0).astype(BF)


def unstacked(rows):
    n = rows.shape[0] // PER_GROUP
    lane = lax.broadcasted_iota(jnp.int32, (n, WIDE), 1) // HEAD
    total = jnp.zeros((n, WIDE), F32)
    for a in range(PER_GROUP):
        total = jnp.where(lane == a, rows[a * n : (a + 1) * n], total)
    return total


def folded(parts):
    sums = []
    for part in parts:
        half = part[:, :128] + part[:, 128:]
        sums.append(half + pltpu.roll(half, HEAD, 1))
    lane = lax.broadcasted_iota(jnp.int32, sums[0].shape, 1)
    return jnp.concatenate(
        [jnp.where(lane < HEAD, sums[0], sums[1]), jnp.where(lane < HEAD, sums[2], sums[3])], axis=1
    )


def centred(scores_sum_axis, probs, products):
    total = jnp.sum(products, axis=scores_sum_axis, keepdims=True)
    return ((products - probs * total) * SCALE).astype(BF)


def group_columns(g):
    return slice(g * WIDE, (g + 1) * WIDE)


def loads(pairs, sems):
    copies = [pltpu.make_async_copy(src, dst, sems.at[i]) for i, (src, dst) in enumerate(pairs)]
    for copy in copies:
        copy.start()
    return copies


def token_kernel(
    place, mem_hbm, tok_hbm, gout_hbm, gain_hbm, own_hbm, other_hbm,
    normed_out, qg_out, part_out, kvp_out, w_out, wo_out, mem, tok, gout, gain, sems
):
    core = place[1]
    near = [(mem_hbm, mem), (tok_hbm, tok), (gain_hbm, gain)]
    first, second = [], []
    inner, outer = slice(0, D + 2 * KV), slice(D + 2 * KV, 2 * D + 2 * KV)
    for i in range(own_hbm.shape[0]):
        for source, side in ((own_hbm, core), (other_hbm, 1 - core)):
            first.append((source.at[i, :, :, inner], w_out.at[:, i, side]))
            second.append((source.at[i, :, :, outer], wo_out.at[:, i, side]))
    copies = loads(near + first + [(gout_hbm, gout)] + second, sems)
    for copy in copies[:3]:
        copy.wait()
    hidden = jnp.concatenate([mem[...].astype(F32), tok[...].astype(F32)], axis=0)
    _, normed = normalised(hidden, gain[...])
    normed_out[...] = normed
    for copy in copies[3 : 3 + len(first)]:
        copy.wait()
    w = w_out[...].reshape(D, D + 2 * KV)
    q = nn(normed[MEM:], w[:, :D])
    kv = nn(normed, w[:, D:]).astype(BF)
    for copy in copies[3 + len(first) :]:
        copy.wait()
    up = nn(gout[...], wo_out[...].reshape(D, D))
    k, v = kv[:, :KV], kv[:, KV:]
    key_at = lax.broadcasted_iota(jnp.int32, (ROWS, PER_GROUP * TOK), 0)
    row_at = lax.broadcasted_iota(jnp.int32, (ROWS, PER_GROUP * TOK), 1) % TOK
    seen = key_at <= row_at + MEM
    key_parts, value_parts = [], []
    for pair in ((0, 1), (2, 3)):
        zqs = [stacked(q[:, group_columns(g)]) for g in pair]
        zus = [stacked(up[:, group_columns(g)]) for g in pair]
        kreps, vreps = [repeated(k, g) for g in pair], [repeated(v, g) for g in pair]
        raised = [jnp.where(seen, jnp.exp(nt(krep, zq) * SCALE), 0.0) for krep, zq in zip(kreps, zqs)]
        products = [nt(vrep, zu) for vrep, zu in zip(vreps, zus)]
        probs = [r * (1.0 / jnp.sum(r, axis=0, keepdims=True)) for r in raised]
        score_grads = [centred(0, p, p * product) for p, product in zip(probs, products)]
        value_parts += [nn(p.astype(BF), zu) for p, zu in zip(probs, zus)]
        key_parts += [nn(grad, zq) for grad, zq in zip(score_grads, zqs)]
        for g, grad, krep in zip(pair, score_grads, kreps):
            qg_out[:, group_columns(g)] = unstacked(tn(grad, krep)).astype(BF)
    part = jnp.concatenate([folded(key_parts), folded(value_parts)], axis=1)
    part_out[...] = part
    kvp_out[:MEM, :] = part[:MEM].astype(BF)
    kvp_out[MEM:ROWS, :] = kv[MEM:]
    kvp_out[ROWS : ROWS + MEM, :] = mem[:, : D // 2]
    kvp_out[ROWS + MEM :, :] = mem[:, D // 2 :]


def mix_kernel(last_hbm, gain_hbm, w, wo, wt, mixed_out, u_out, last, gain, sems):
    for copy in loads([(last_hbm, last), (gain_hbm, gain)], sems):
        copy.wait()
    u_out[...] = nn(last[...], wo[...]).astype(BF)
    wt[...] = w[...].T
    scaled = (wt[...].astype(F32) * gain[...]).astype(BF)
    mixed_out[...] = nn(scaled, wo[...]).astype(BF)


def ready_kernel(place, gain, w, wo, *refs):
    parts, refs = refs[:SPAN], refs[SPAN:]
    probs_k_out, probs_q_out, krep_out, vrep_out, zq_out, near_out, mem_out, qkv_out, hw_out, inv_out = refs
    slots = [(place[0] + ahead) % SPAN for ahead in range(SPAN)]
    spans = [pl.ds(pl.multiple_of(s * MEM, MEM), MEM) for s in slots]
    for rows, kvp in zip(spans, parts):
        mem_out[rows, :] = jnp.concatenate([kvp[ROWS : ROWS + MEM, :], kvp[ROWS + MEM :, :]], axis=1)
        near_out[rows, :] = kvp[:MEM, :].astype(F32)
    inverse, normed = normalised(mem_out[...].astype(F32), gain[...])
    inv_out[...] = inverse
    hw_out[...] = nn(mem_out[...], wo[...])
    qkv_out[...] = nn(normed, w[...])
    for s, rows, kvp in zip(slots, spans, parts):
        qkv = qkv_out[rows, :]
        k = jnp.concatenate([qkv[:, D : D + KV].astype(BF), kvp[MEM:ROWS, :KV]], axis=0)
        v = jnp.concatenate([qkv[:, D + KV :].astype(BF), kvp[MEM:ROWS, KV:]], axis=0)
        zqs = [stacked(qkv[:, group_columns(g)]) for g in range(GROUPS)]
        kreps = [repeated(k, g) for g in range(GROUPS)]
        raised_k = [jnp.exp(nt(krep, zq) * SCALE) for krep, zq in zip(kreps, zqs)]
        raised_q = [jnp.exp(nt(zq, krep) * SCALE) for krep, zq in zip(kreps, zqs)]
        for g in range(GROUPS):
            at = s * GROUPS + g
            probs_k_out[at] = raised_k[g] * (1.0 / jnp.sum(raised_k[g], axis=0, keepdims=True))
            probs_q_out[at] = raised_q[g] * (1.0 / jnp.sum(raised_q[g], axis=1, keepdims=True))
            krep_out[at] = kreps[g]
            vrep_out[at] = repeated(v, g)
            zq_out[at] = zqs[g]


def chain_kernel(
    turn, place, arrived, before, mixed, probs_k, probs_q, krep, vrep, zq, qkv4, hw4, inv4, near, send_out, u_out, grads_out
):
    up = arrived[...].astype(F32)
    if turn > 0:
        up = jnp.where(place[2] == turn, up, before[(SPAN - 1) * MEM :, :].astype(F32))
    for s in reversed(range(SPAN)):
        rows = slice(s * MEM, (s + 1) * MEM)
        u_out[rows, :] = up.astype(BF)
        ats = range(s * GROUPS, (s + 1) * GROUPS)
        zus = [stacked(up[:, group_columns(g)]) for g in range(GROUPS)]
        by_query = [probs_q[at] * nt(zu, vrep[at]) for at, zu in zip(ats, zus)]
        by_key = [probs_k[at] * nt(vrep[at], zu) for at, zu in zip(ats, zus)]
        value_parts = [nn(probs_k[at, :MEM].astype(BF), zu) for at, zu in zip(ats, zus)]
        score_grads = [centred(1, probs_q[at], products) for at, products in zip(ats, by_query)]
        totals = [jnp.sum(products, axis=0, keepdims=True) for products in by_key]
        near_grads = [
            ((products[:MEM] - probs_k[at, :MEM] * total) * SCALE).astype(BF)
            for at, products, total in zip(ats, by_key, totals)
        ]
        query_grads = [unstacked(nn(grad, krep[at])) for at, grad in zip(ats, score_grads)]
        key_parts = [nn(grad, zq[at]) for at, grad in zip(ats, near_grads)]
        kv_grad = jnp.concatenate([folded(key_parts), folded(value_parts)], axis=1) + near[rows, :]
        grads = jnp.concatenate(query_grads + [kv_grad], axis=1).astype(BF)
        grads_out[rows, :] = grads
        inverse = inv4[rows, :]
        along = jnp.sum(grads.astype(F32) * qkv4[rows, :], axis=-1, keepdims=True) * (inverse * inverse / D)
        up = up + inverse * nn(grads, mixed[...]) - along * hw4[rows, :]
    send_out[...] = up.astype(BF)


def weight_kernel(place, u4, probs, krep, vrep, zq, part, normed, kv_out, mine_out, other_out):
    r = place[0]
    up = u4[pl.ds(pl.multiple_of(r * MEM, MEM), MEM), :]
    ats = [r * GROUPS + g for g in range(GROUPS)]
    zus = [stacked(up[:, group_columns(g)]) for g in range(GROUPS)]
    ps = [probs[at] for at in ats]
    products = [p * nt(vrep[at], zu) for at, p, zu in zip(ats, ps, zus)]
    value_parts = [nn(p.astype(BF), zu) for p, zu in zip(ps, zus)]
    score_grads = [centred(0, p, product) for p, product in zip(ps, products)]
    key_parts = [nn(grad, zq[at]) for at, grad in zip(ats, score_grads)]
    kv_grad = jnp.concatenate([folded(key_parts), folded(value_parts)], axis=1) + part[...]
    kv_grad = kv_grad.astype(BF)
    kv_out[...] = kv_grad
    grad = tn(normed[...], kv_grad)
    pieces, depth, _ = mine_out.shape
    share = 8 * pieces
    first = place[1] == 0
    for piece in range(pieces):
        halves = [
            jnp.concatenate([grad[at : at + 8] for at in range(core * share + piece * 8, D, 2 * share)], axis=0)
            for core in range(2)
        ]
        mine_out[piece] = jnp.where(first, halves[0], halves[1]).astype(BF)
        other_out[piece] = jnp.where(first, halves[1], halves[0]).astype(BF)


def memory_kernel(turn, place, arrived, held, grads4, wt, mem4, inv4, gain, *outs):
    current = arrived[...].astype(F32)
    if turn > 0:
        current = jnp.where(place[2] == turn, current, held[...].astype(F32))
    hidden, inverse = mem4[...].astype(F32), inv4[...]
    change = norm_backward(0.0, nn(grads4[...], wt[...]), hidden, inverse, gain[...])
    if len(outs) > 1:
        outs[1][...] = current.astype(BF)
        for s in range(SPAN):
            current = current + change[s * MEM : (s + 1) * MEM]
        outs[0][...] = current.astype(BF)
        return
    own = current
    for s in reversed(range(SPAN)):
        current = current + change[s * MEM : (s + 1) * MEM]
        own = jnp.where(place[0] == s, current, own)
    outs[0][...] = own.astype(BF)


def rows_kernel(tok_hbm, gout_hbm, gain_hbm, qg_hbm, kv_hbm, wt, out, tok, gout, gain, qg, kv_grad, sems):
    pairs = [(tok_hbm, tok), (gain_hbm, gain), (qg_hbm, qg), (kv_hbm, kv_grad), (gout_hbm, gout)]
    for copy in loads(pairs, sems):
        copy.wait()
    hidden = tok[...].astype(F32)
    inverse, _ = normalised(hidden, gain[...])
    normed_grad = nn(qg[...], wt[:D, :]) + nn(kv_grad[MEM:, :], wt[D:, :])
    out[...] = norm_backward(gout[...].astype(F32), normed_grad, hidden, inverse, gain[...]).astype(BF)


def call(kernel, outs, args, flops, scalars=0, far=0, scratch=()):
    vmem = pl.BlockSpec(memory_space=pltpu.VMEM)
    smem = pl.BlockSpec(memory_space=pltpu.SMEM)
    hbm = pl.BlockSpec(memory_space=pltpu.HBM)
    args = [
        pltpu.with_memory_space_constraint(a, pltpu.HBM) if scalars <= i < scalars + far else a for i, a in enumerate(args)
    ]
    moved = sum(a.size * a.dtype.itemsize for a in args) + sum(o.size * o.dtype.itemsize for o in outs)
    return pl.pallas_call(
        kernel,
        out_shape=outs,
        in_specs=[smem] * scalars + [hbm] * far + [vmem] * (len(args) - scalars - far),
        out_specs=[vmem] * len(outs),
        scratch_shapes=list(scratch),
        compiler_params=pltpu.CompilerParams(vmem_limit_bytes=20 * 1024 * 1024),
        cost_estimate=pl.CostEstimate(flops=flops, bytes_accessed=moved, transcendentals=0),
    )(*args)


def shape(dims, dtype=BF):
    return jax.ShapeDtypeStruct(dims, dtype)


def runs(axis_size, length, stride):
    block = length * stride
    return [
        [b + o + i * stride for i in range(length)] for b in range(0, axis_size, block) for o in range(stride)
    ]


def gathered(shard):
    docs = lax.axis_size("dp")
    block = lax.all_gather(shard, "dp", axis=0, axis_index_groups=runs(docs, docs // 8, 8))
    copies = jnp.broadcast_to(block[None], (4,) + block.shape)
    own = lax.all_to_all(copies, "dp", 0, 0, tiled=True, axis_index_groups=runs(docs, 4, 2))
    return own, lax.ppermute(own, "dp", [(i, i ^ 1) for i in range(docs)])


def summed_over_group(mine, other):
    docs = lax.axis_size("dp")
    got = lax.ppermute(other, "dp", [(i, i ^ 1) for i in range(docs)])
    block = (mine.astype(F32) + got.astype(F32)).astype(BF)
    block = lax.all_to_all(block, "seg", 0, 0, tiled=True, axis_index_groups=runs(lax.axis_size("seg"), SPAN, 1))
    return jnp.sum(block.astype(F32), axis=0).astype(BF)


def summed_over_documents(block):
    docs = lax.axis_size("dp")
    chunks = docs // 2
    block = block.reshape(chunks, 8, 2 * KV)
    block = lax.all_to_all(block, "dp", 0, 0, tiled=True, axis_index_groups=runs(docs, chunks, 2))
    return jnp.sum(block.astype(F32), axis=0).astype(BF)


def summed_over_segments(block):
    n_seg = lax.axis_size("seg")
    copies = jnp.broadcast_to(block[None], (n_seg,) + block.shape)
    got = lax.all_to_all(copies, "seg", 0, 0, tiled=True).reshape(n_seg // SPAN, SPAN, 8, 2 * KV)
    return jnp.sum(got.astype(F32), axis=0).reshape(SPAN * 8, 2 * KV)


def body(tokens, grad_output, memories, grad_last, norm_gain, query_weight, key_weight, value_weight, out_weight):
    position = lax.axis_index("seg")
    n_seg = lax.axis_size("seg")
    docs = lax.axis_size("dp")
    turns = n_seg // SPAN
    tok, gout, mem, last, gain = tokens[0], grad_output[0], memories[0, 0], grad_last[0], norm_gain[None]
    block = position // SPAN
    place = jnp.stack([position % SPAN, lax.axis_index("dp") % 2, turns - 1 - block]).astype(jnp.int32)

    weights = gathered(jnp.concatenate([query_weight, key_weight, value_weight, out_weight.T], axis=1))
    *weights, place = lax.optimization_barrier((*weights, place))

    dma = pltpu.SemaphoreType.DMA
    normed, qg, part, kvp, w, wo = call(
        token_kernel,
        [
            shape((ROWS, D)),
            shape((TOK, D)),
            shape((ROWS, 2 * KV), F32),
            shape((ROWS + 2 * MEM, 2 * KV)),
            shape((docs // 8, 4, 2, D // docs, D + 2 * KV)),
            shape((docs // 8, 4, 2, D // docs, D)),
        ],
        (place, mem, tok, gout, gain, *weights),
        1_500_000_000,
        scalars=1,
        far=6,
        scratch=(
            pltpu.VMEM((MEM, D), BF),
            pltpu.VMEM((TOK, D), BF),
            pltpu.VMEM((TOK, D), BF),
            pltpu.VMEM((1, D), F32),
            dma((4 + 16,)),
        ),
    )
    w, wo = w.reshape(D, D + 2 * KV), wo.reshape(D, D)
    kvps = [kvp]
    for ahead in range(1, SPAN):
        route = [(i, i // SPAN * SPAN + (i - ahead) % SPAN) for i in range(n_seg)]
        kvps.append(lax.ppermute(kvp, "seg", route))
    wt, mixed, arrived = call(
        mix_kernel,
        [shape((D + 2 * KV, D)), shape((D + 2 * KV, D)), shape((MEM, D))],
        (last, gain, w, wo),
        4_000_000_000,
        far=2,
        scratch=(pltpu.VMEM((MEM, D), BF), pltpu.VMEM((1, D), F32), dma((2,))),
    )
    count = SPAN * GROUPS
    probs_k, probs_q, krep, vrep, zq, near, mem4, qkv4, hw4, inv4 = call(
        ready_kernel,
        [
            shape((count, ROWS, PER_GROUP * MEM), F32),
            shape((count, PER_GROUP * MEM, ROWS), F32),
            shape((count, ROWS, WIDE)),
            shape((count, ROWS, WIDE)),
            shape((count, PER_GROUP * MEM, WIDE)),
            shape((SPAN * MEM, 2 * KV), F32),
            shape((SPAN * MEM, D)),
            shape((SPAN * MEM, D + 2 * KV), F32),
            shape((SPAN * MEM, D), F32),
            shape((SPAN * MEM, 1), F32),
        ],
        (place, gain, w, wo, *kvps),
        400_000_000,
        scalars=1,
    )
    u4 = arrived
    memory_arrived = memory_held = last
    for turn in range(turns):
        send, u4, grads4 = call(
            functools.partial(chain_kernel, turn),
            [shape((MEM, D)), shape((SPAN * MEM, D)), shape((SPAN * MEM, D + 2 * KV))],
            (place, arrived, u4, mixed, probs_k, probs_q, krep, vrep, zq, qkv4, hw4, inv4, near),
            1_000_000_000,
            scalars=1,
        )
        if turn < turns - 1:
            route = [(i, i - SPAN) for i in range((turns - 1 - turn) * SPAN, (turns - turn) * SPAN)]
            arrived = lax.ppermute(send, "seg", route)
            memory_send, memory_held = call(
                functools.partial(memory_kernel, turn),
                [shape((MEM, D)), shape((MEM, D))],
                (place, memory_arrived, memory_held, grads4, wt, mem4, inv4, gain),
                400_000_000,
                scalars=1,
            )
            arrived, memory_send = lax.optimization_barrier((arrived, memory_send))
            memory_arrived = lax.ppermute(memory_send, "seg", route)
    half = (SPAN, docs // 2 * 8, 2 * KV)
    kv_grad, mine, other = call(
        weight_kernel,
        [shape((ROWS, 2 * KV)), shape(half), shape(half)],
        (place, u4, probs_k, krep, vrep, zq, part, normed),
        400_000_000,
        scalars=1,
    )
    (grad_memories,) = call(
        functools.partial(memory_kernel, turns - 1),
        [shape((MEM, D))],
        (place, memory_arrived, memory_held, grads4, wt, mem4, inv4, gain),
        400_000_000,
        scalars=1,
    )
    (grad_tokens,) = call(
        rows_kernel,
        [shape((TOK, D))],
        (tok, gout, gain, qg, kv_grad, wt),
        500_000_000,
        far=5,
        scratch=(
            pltpu.VMEM((TOK, D), BF),
            pltpu.VMEM((TOK, D), BF),
            pltpu.VMEM((1, D), F32),
            pltpu.VMEM((TOK, D), BF),
            pltpu.VMEM((ROWS, 2 * KV), BF),
            dma((5,)),
        ),
    )
    block = summed_over_group(mine, other)
    block = summed_over_documents(block)
    block, grad_tokens, grad_memories = lax.optimization_barrier((block, grad_tokens, grad_memories))
    total = summed_over_segments(block) / docs
    return (grad_tokens[None], grad_memories[None, None], total[:, :KV], total[:, KV:])


def solution(mesh):
    in_specs = (
        P("dp", "seg", None),
        P("dp", "seg", None),
        P("dp", "seg", None, None),
        P("dp", None, None),
        P(),
        P("dp", None),
        P("dp", None),
        P("dp", None),
        P(None, "dp"),
    )
    out_specs = (P("dp", "seg", None), P("dp", "seg", None, None), P("dp", None), P("dp", None))
    return jax.shard_map(body, mesh=mesh, in_specs=in_specs, out_specs=out_specs, check_vma=False)
```

```python
import functools

import jax
import jax.numpy as jnp
from jax import lax
from jax.experimental import pallas as pl
from jax.experimental.pallas import tpu as pltpu
from jax.sharding import PartitionSpec as P

D = 1024
GROUPS = 4
PER_GROUP = 4
HEAD = 64
WIDE = PER_GROUP * HEAD
KV = GROUPS * HEAD
MEM = 32
TOK = 128
ROWS = MEM + TOK
SPAN = 4
EPS = 1e-05
SCALE = 0.125
BF = jnp.bfloat16
F32 = jnp.float32


def nn(a, b):
    return lax.dot_general(a, b, (((1,), (0,)), ((), ())), preferred_element_type=F32)


def nt(a, b):
    return lax.dot_general(a, b, (((1,), (1,)), ((), ())), preferred_element_type=F32)


def tn(a, b):
    return lax.dot_general(a, b, (((0,), (0,)), ((), ())), preferred_element_type=F32)


def normalised(rows, gain):
    inverse = lax.rsqrt(jnp.mean(rows * rows, axis=-1, keepdims=True) + EPS)
    return inverse, (rows * inverse * gain).astype(BF)


def norm_backward(cotangent, normed_grad, hidden, inverse, gain):
    scaled = normed_grad * gain
    mean = jnp.mean(scaled * hidden, axis=-1, keepdims=True)
    return cotangent + inverse * (scaled - hidden * (inverse * inverse * mean))


def repeated(rows, g):
    half = rows[:, (g // 2) * 128 : (g // 2) * 128 + 128].astype(F32)
    lane = lax.broadcasted_iota(jnp.int32, half.shape, 1)
    kept = jnp.where((lane < HEAD) == (g % 2 == 0), half, 0.0)
    both = kept + pltpu.roll(kept, HEAD, 1)
    return jnp.concatenate([both, both], axis=1).astype(BF)


def stacked(rows):
    rows = rows.astype(F32)
    lane = lax.broadcasted_iota(jnp.int32, rows.shape, 1) // HEAD
    return jnp.concatenate([jnp.where(lane == a, rows, 0.0) for a in range(PER_GROUP)], axis=0).astype(BF)


def unstacked(rows):
    n = rows.shape[0] // PER_GROUP
    lane = lax.broadcasted_iota(jnp.int32, (n, WIDE), 1) // HEAD
    total = jnp.zeros((n, WIDE), F32)
    for a in range(PER_GROUP):
        total = jnp.where(lane == a, rows[a * n : (a + 1) * n], total)
    return total


def folded(parts):
    sums = []
    for part in parts:
        half = part[:, :128] + part[:, 128:]
        sums.append(half + pltpu.roll(half, HEAD, 1))
    lane = lax.broadcasted_iota(jnp.int32, sums[0].shape, 1)
    return jnp.concatenate(
        [jnp.where(lane < HEAD, sums[0], sums[1]), jnp.where(lane < HEAD, sums[2], sums[3])], axis=1
    )


def centred(scores_sum_axis, probs, products):
    total = jnp.sum(products, axis=scores_sum_axis, keepdims=True)
    return ((products - probs * total) * SCALE).astype(BF)


def group_columns(g):
    return slice(g * WIDE, (g + 1) * WIDE)


def loads(pairs, sems):
    copies = [pltpu.make_async_copy(src, dst, sems.at[i]) for i, (src, dst) in enumerate(pairs)]
    for copy in copies:
        copy.start()
    return copies


def token_kernel(
    place, mem_hbm, tok_hbm, gout_hbm, gain_hbm, own_hbm, other_hbm,
    normed_out, qg_out, part_out, kvp_out, w_out, wo_out, mem, tok, gout, gain, sems
):
    core = place[1]
    near = [(mem_hbm, mem), (tok_hbm, tok), (gain_hbm, gain)]
    first, second = [], []
    inner, outer = slice(0, D + 2 * KV), slice(D + 2 * KV, 2 * D + 2 * KV)
    for i in range(own_hbm.shape[0]):
        for source, side in ((own_hbm, core), (other_hbm, 1 - core)):
            first.append((source.at[i, :, :, inner], w_out.at[:, i, side]))
            second.append((source.at[i, :, :, outer], wo_out.at[:, i, side]))
    copies = loads(near + first + [(gout_hbm, gout)] + second, sems)
    for copy in copies[:3]:
        copy.wait()
    hidden = jnp.concatenate([mem[...].astype(F32), tok[...].astype(F32)], axis=0)
    _, normed = normalised(hidden, gain[...])
    normed_out[...] = normed
    for copy in copies[3 : 3 + len(first)]:
        copy.wait()
    w = w_out[...].reshape(D, D + 2 * KV)
    q = nn(normed[MEM:], w[:, :D])
    kv = nn(normed, w[:, D:]).astype(BF)
    for copy in copies[3 + len(first) :]:
        copy.wait()
    up = nn(gout[...], wo_out[...].reshape(D, D))
    k, v = kv[:, :KV], kv[:, KV:]
    key_at = lax.broadcasted_iota(jnp.int32, (ROWS, PER_GROUP * TOK), 0)
    row_at = lax.broadcasted_iota(jnp.int32, (ROWS, PER_GROUP * TOK), 1) % TOK
    seen = key_at <= row_at + MEM
    key_parts, value_parts = [], []
    for pair in ((0, 1), (2, 3)):
        zqs = [stacked(q[:, group_columns(g)]) for g in pair]
        zus = [stacked(up[:, group_columns(g)]) for g in pair]
        kreps, vreps = [repeated(k, g) for g in pair], [repeated(v, g) for g in pair]
        raised = [jnp.where(seen, jnp.exp(nt(krep, zq) * SCALE), 0.0) for krep, zq in zip(kreps, zqs)]
        products = [nt(vrep, zu) for vrep, zu in zip(vreps, zus)]
        probs = [r * (1.0 / jnp.sum(r, axis=0, keepdims=True)) for r in raised]
        score_grads = [centred(0, p, p * product) for p, product in zip(probs, products)]
        value_parts += [nn(p.astype(BF), zu) for p, zu in zip(probs, zus)]
        key_parts += [nn(grad, zq) for grad, zq in zip(score_grads, zqs)]
        for g, grad, krep in zip(pair, score_grads, kreps):
            qg_out[:, group_columns(g)] = unstacked(tn(grad, krep)).astype(BF)
    part = jnp.concatenate([folded(key_parts), folded(value_parts)], axis=1)
    part_out[...] = part
    kvp_out[:MEM, :] = part[:MEM].astype(BF)
    kvp_out[MEM:ROWS, :] = kv[MEM:]
    kvp_out[ROWS : ROWS + MEM, :] = mem[:, : D // 2]
    kvp_out[ROWS + MEM :, :] = mem[:, D // 2 :]


def mix_kernel(last_hbm, gain_hbm, w, wo, wt, mixed_out, u_out, last, gain, sems):
    for copy in loads([(last_hbm, last), (gain_hbm, gain)], sems):
        copy.wait()
    u_out[...] = nn(last[...], wo[...]).astype(BF)
    wt[...] = w[...].T
    scaled = (wt[...].astype(F32) * gain[...]).astype(BF)
    mixed_out[...] = nn(scaled, wo[...]).astype(BF)


def ready_kernel(place, gain, w, wo, *refs):
    parts, refs = refs[:SPAN], refs[SPAN:]
    probs_k_out, probs_q_out, krep_out, vrep_out, zq_out, near_out, mem_out, qkv_out, hw_out, inv_out = refs
    slots = [(place[0] + ahead) % SPAN for ahead in range(SPAN)]
    spans = [pl.ds(pl.multiple_of(s * MEM, MEM), MEM) for s in slots]
    for rows, kvp in zip(spans, parts):
        mem_out[rows, :] = jnp.concatenate([kvp[ROWS : ROWS + MEM, :], kvp[ROWS + MEM :, :]], axis=1)
        near_out[rows, :] = kvp[:MEM, :].astype(F32)
    inverse, normed = normalised(mem_out[...].astype(F32), gain[...])
    inv_out[...] = inverse
    hw_out[...] = nn(mem_out[...], wo[...])
    qkv_out[...] = nn(normed, w[...])
    for s, rows, kvp in zip(slots, spans, parts):
        qkv = qkv_out[rows, :]
        k = jnp.concatenate([qkv[:, D : D + KV].astype(BF), kvp[MEM:ROWS, :KV]], axis=0)
        v = jnp.concatenate([qkv[:, D + KV :].astype(BF), kvp[MEM:ROWS, KV:]], axis=0)
        zqs = [stacked(qkv[:, group_columns(g)]) for g in range(GROUPS)]
        kreps = [repeated(k, g) for g in range(GROUPS)]
        raised_k = [jnp.exp(nt(krep, zq) * SCALE) for krep, zq in zip(kreps, zqs)]
        raised_q = [jnp.exp(nt(zq, krep) * SCALE) for krep, zq in zip(kreps, zqs)]
        for g in range(GROUPS):
            at = s * GROUPS + g
            probs_k_out[at] = raised_k[g] * (1.0 / jnp.sum(raised_k[g], axis=0, keepdims=True))
            probs_q_out[at] = raised_q[g] * (1.0 / jnp.sum(raised_q[g], axis=1, keepdims=True))
            krep_out[at] = kreps[g]
            vrep_out[at] = repeated(v, g)
            zq_out[at] = zqs[g]


def chain_kernel(
    turn, place, arrived, before, mixed, probs_k, probs_q, krep, vrep, zq, qkv4, hw4, inv4, near, send_out, u_out, grads_out
):
    up = arrived[...].astype(F32)
    if turn > 0:
        up = jnp.where(place[2] == turn, up, before[(SPAN - 1) * MEM :, :].astype(F32))
    for s in reversed(range(SPAN)):
        rows = slice(s * MEM, (s + 1) * MEM)
        u_out[rows, :] = up.astype(BF)
        ats = range(s * GROUPS, (s + 1) * GROUPS)
        zus = [stacked(up[:, group_columns(g)]) for g in range(GROUPS)]
        by_query = [probs_q[at] * nt(zu, vrep[at]) for at, zu in zip(ats, zus)]
        by_key = [probs_k[at] * nt(vrep[at], zu) for at, zu in zip(ats, zus)]
        value_parts = [nn(probs_k[at, :MEM].astype(BF), zu) for at, zu in zip(ats, zus)]
        score_grads = [centred(1, probs_q[at], products) for at, products in zip(ats, by_query)]
        totals = [jnp.sum(products, axis=0, keepdims=True) for products in by_key]
        near_grads = [
            ((products[:MEM] - probs_k[at, :MEM] * total) * SCALE).astype(BF)
            for at, products, total in zip(ats, by_key, totals)
        ]
        query_grads = [unstacked(nn(grad, krep[at])) for at, grad in zip(ats, score_grads)]
        key_parts = [nn(grad, zq[at]) for at, grad in zip(ats, near_grads)]
        kv_grad = jnp.concatenate([folded(key_parts), folded(value_parts)], axis=1) + near[rows, :]
        grads = jnp.concatenate(query_grads + [kv_grad], axis=1).astype(BF)
        grads_out[rows, :] = grads
        inverse = inv4[rows, :]
        along = jnp.sum(grads.astype(F32) * qkv4[rows, :], axis=-1, keepdims=True) * (inverse * inverse / D)
        up = up + inverse * nn(grads, mixed[...]) - along * hw4[rows, :]
    send_out[...] = up.astype(BF)


def weight_kernel(place, u4, probs, krep, vrep, zq, part, normed, kv_out, mine_out, other_out):
    r = place[0]
    up = u4[pl.ds(pl.multiple_of(r * MEM, MEM), MEM), :]
    ats = [r * GROUPS + g for g in range(GROUPS)]
    zus = [stacked(up[:, group_columns(g)]) for g in range(GROUPS)]
    ps = [probs[at] for at in ats]
    products = [p * nt(vrep[at], zu) for at, p, zu in zip(ats, ps, zus)]
    value_parts = [nn(p.astype(BF), zu) for p, zu in zip(ps, zus)]
    score_grads = [centred(0, p, product) for p, product in zip(ps, products)]
    key_parts = [nn(grad, zq[at]) for at, grad in zip(ats, score_grads)]
    kv_grad = jnp.concatenate([folded(key_parts), folded(value_parts)], axis=1) + part[...]
    kv_grad = kv_grad.astype(BF)
    kv_out[...] = kv_grad
    grad = tn(normed[...], kv_grad)
    pieces, depth, _ = mine_out.shape
    share = 8 * pieces
    first = place[1] == 0
    for piece in range(pieces):
        halves = [
            jnp.concatenate([grad[at : at + 8] for at in range(core * share + piece * 8, D, 2 * share)], axis=0)
            for core in range(2)
        ]
        mine_out[piece] = jnp.where(first, halves[0], halves[1]).astype(BF)
        other_out[piece] = jnp.where(first, halves[1], halves[0]).astype(BF)


def memory_kernel(turn, place, arrived, held, grads4, wt, mem4, inv4, gain, *outs):
    current = arrived[...].astype(F32)
    if turn > 0:
        current = jnp.where(place[2] == turn, current, held[...].astype(F32))
    hidden, inverse = mem4[...].astype(F32), inv4[...]
    change = norm_backward(0.0, nn(grads4[...], wt[...]), hidden, inverse, gain[...])
    if len(outs) > 1:
        outs[1][...] = current.astype(BF)
        for s in range(SPAN):
            current = current + change[s * MEM : (s + 1) * MEM]
        outs[0][...] = current.astype(BF)
        return
    own = current
    for s in reversed(range(SPAN)):
        current = current + change[s * MEM : (s + 1) * MEM]
        own = jnp.where(place[0] == s, current, own)
    outs[0][...] = own.astype(BF)


def rows_kernel(tok_hbm, gout_hbm, gain_hbm, qg_hbm, kv_hbm, wt, out, tok, gout, gain, qg, kv_grad, sems):
    pairs = [(tok_hbm, tok), (gain_hbm, gain), (qg_hbm, qg), (kv_hbm, kv_grad), (gout_hbm, gout)]
    for copy in loads(pairs, sems):
        copy.wait()
    hidden = tok[...].astype(F32)
    inverse, _ = normalised(hidden, gain[...])
    normed_grad = nn(qg[...], wt[:D, :]) + nn(kv_grad[MEM:, :], wt[D:, :])
    out[...] = norm_backward(gout[...].astype(F32), normed_grad, hidden, inverse, gain[...]).astype(BF)


def call(kernel, outs, args, flops, scalars=0, far=0, scratch=()):
    vmem = pl.BlockSpec(memory_space=pltpu.VMEM)
    smem = pl.BlockSpec(memory_space=pltpu.SMEM)
    hbm = pl.BlockSpec(memory_space=pltpu.HBM)
    args = [
        pltpu.with_memory_space_constraint(a, pltpu.HBM) if scalars <= i < scalars + far else a for i, a in enumerate(args)
    ]
    moved = sum(a.size * a.dtype.itemsize for a in args) + sum(o.size * o.dtype.itemsize for o in outs)
    return pl.pallas_call(
        kernel,
        out_shape=outs,
        in_specs=[smem] * scalars + [hbm] * far + [vmem] * (len(args) - scalars - far),
        out_specs=[vmem] * len(outs),
        scratch_shapes=list(scratch),
        compiler_params=pltpu.CompilerParams(vmem_limit_bytes=20 * 1024 * 1024),
        cost_estimate=pl.CostEstimate(flops=flops, bytes_accessed=moved, transcendentals=0),
    )(*args)


def shape(dims, dtype=BF):
    return jax.ShapeDtypeStruct(dims, dtype)


def runs(axis_size, length, stride):
    block = length * stride
    return [
        [b + o + i * stride for i in range(length)] for b in range(0, axis_size, block) for o in range(stride)
    ]


def gathered(shard):
    docs = lax.axis_size("dp")
    block = lax.all_gather(shard, "dp", axis=0, axis_index_groups=runs(docs, docs // 8, 8))
    copies = jnp.broadcast_to(block[None], (4,) + block.shape)
    own = lax.all_to_all(copies, "dp", 0, 0, tiled=True, axis_index_groups=runs(docs, 4, 2))
    return own, lax.ppermute(own, "dp", [(i, i ^ 1) for i in range(docs)])


def summed_over_group(mine, other):
    docs = lax.axis_size("dp")
    got = lax.ppermute(other, "dp", [(i, i ^ 1) for i in range(docs)])
    block = (mine.astype(F32) + got.astype(F32)).astype(BF)
    block = lax.all_to_all(block, "seg", 0, 0, tiled=True, axis_index_groups=runs(lax.axis_size("seg"), SPAN, 1))
    total = block[0].astype(F32)
    for member in range(1, SPAN):
        total = total + block[member].astype(F32)
    return total.astype(BF)


def summed_over_documents(block):
    docs = lax.axis_size("dp")
    chunks = docs // 2
    block = block.reshape(chunks, 8, 2 * KV)
    block = lax.all_to_all(block, "dp", 0, 0, tiled=True, axis_index_groups=runs(docs, chunks, 2))
    return jnp.sum(block.astype(F32), axis=0).astype(BF)


def summed_over_segments(block):
    n_seg = lax.axis_size("seg")
    copies = jnp.broadcast_to(block[None], (n_seg,) + block.shape)
    got = lax.all_to_all(copies, "seg", 0, 0, tiled=True).reshape(n_seg // SPAN, SPAN, 8, 2 * KV)
    return jnp.sum(got.astype(F32), axis=0).reshape(SPAN * 8, 2 * KV)


def body(tokens, grad_output, memories, grad_last, norm_gain, query_weight, key_weight, value_weight, out_weight):
    position = lax.axis_index("seg")
    n_seg = lax.axis_size("seg")
    docs = lax.axis_size("dp")
    turns = n_seg // SPAN
    tok, gout, mem, last, gain = tokens[0], grad_output[0], memories[0, 0], grad_last[0], norm_gain[None]
    block = position // SPAN
    place = jnp.stack([position % SPAN, lax.axis_index("dp") % 2, turns - 1 - block]).astype(jnp.int32)

    weights = gathered(jnp.concatenate([query_weight, key_weight, value_weight, out_weight.T], axis=1))
    *weights, place = lax.optimization_barrier((*weights, place))

    dma = pltpu.SemaphoreType.DMA
    normed, qg, part, kvp, w, wo = call(
        token_kernel,
        [
            shape((ROWS, D)),
            shape((TOK, D)),
            shape((ROWS, 2 * KV), F32),
            shape((ROWS + 2 * MEM, 2 * KV)),
            shape((docs // 8, 4, 2, D // docs, D + 2 * KV)),
            shape((docs // 8, 4, 2, D // docs, D)),
        ],
        (place, mem, tok, gout, gain, *weights),
        1_500_000_000,
        scalars=1,
        far=6,
        scratch=(
            pltpu.VMEM((MEM, D), BF),
            pltpu.VMEM((TOK, D), BF),
            pltpu.VMEM((TOK, D), BF),
            pltpu.VMEM((1, D), F32),
            dma((4 + 16,)),
        ),
    )
    w, wo = w.reshape(D, D + 2 * KV), wo.reshape(D, D)
    kvps = [kvp]
    for ahead in range(1, SPAN):
        route = [(i, i // SPAN * SPAN + (i - ahead) % SPAN) for i in range(n_seg)]
        kvps.append(lax.ppermute(kvp, "seg", route))
    wt, mixed, arrived = call(
        mix_kernel,
        [shape((D + 2 * KV, D)), shape((D + 2 * KV, D)), shape((MEM, D))],
        (last, gain, w, wo),
        4_000_000_000,
        far=2,
        scratch=(pltpu.VMEM((MEM, D), BF), pltpu.VMEM((1, D), F32), dma((2,))),
    )
    count = SPAN * GROUPS
    probs_k, probs_q, krep, vrep, zq, near, mem4, qkv4, hw4, inv4 = call(
        ready_kernel,
        [
            shape((count, ROWS, PER_GROUP * MEM), F32),
            shape((count, PER_GROUP * MEM, ROWS), F32),
            shape((count, ROWS, WIDE)),
            shape((count, ROWS, WIDE)),
            shape((count, PER_GROUP * MEM, WIDE)),
            shape((SPAN * MEM, 2 * KV), F32),
            shape((SPAN * MEM, D)),
            shape((SPAN * MEM, D + 2 * KV), F32),
            shape((SPAN * MEM, D), F32),
            shape((SPAN * MEM, 1), F32),
        ],
        (place, gain, w, wo, *kvps),
        400_000_000,
        scalars=1,
    )
    u4 = arrived
    memory_arrived = memory_held = last
    for turn in range(turns):
        send, u4, grads4 = call(
            functools.partial(chain_kernel, turn),
            [shape((MEM, D)), shape((SPAN * MEM, D)), shape((SPAN * MEM, D + 2 * KV))],
            (place, arrived, u4, mixed, probs_k, probs_q, krep, vrep, zq, qkv4, hw4, inv4, near),
            1_000_000_000,
            scalars=1,
        )
        if turn < turns - 1:
            route = [(i, i - SPAN) for i in range((turns - 1 - turn) * SPAN, (turns - turn) * SPAN)]
            arrived = lax.ppermute(send, "seg", route)
            memory_send, memory_held = call(
                functools.partial(memory_kernel, turn),
                [shape((MEM, D)), shape((MEM, D))],
                (place, memory_arrived, memory_held, grads4, wt, mem4, inv4, gain),
                400_000_000,
                scalars=1,
            )
            arrived, memory_send = lax.optimization_barrier((arrived, memory_send))
            memory_arrived = lax.ppermute(memory_send, "seg", route)
    half = (SPAN, docs // 2 * 8, 2 * KV)
    kv_grad, mine, other = call(
        weight_kernel,
        [shape((ROWS, 2 * KV)), shape(half), shape(half)],
        (place, u4, probs_k, krep, vrep, zq, part, normed),
        400_000_000,
        scalars=1,
    )
    (grad_memories,) = call(
        functools.partial(memory_kernel, turns - 1),
        [shape((MEM, D))],
        (place, memory_arrived, memory_held, grads4, wt, mem4, inv4, gain),
        400_000_000,
        scalars=1,
    )
    (grad_tokens,) = call(
        rows_kernel,
        [shape((TOK, D))],
        (tok, gout, gain, qg, kv_grad, wt),
        500_000_000,
        far=5,
        scratch=(
            pltpu.VMEM((TOK, D), BF),
            pltpu.VMEM((TOK, D), BF),
            pltpu.VMEM((1, D), F32),
            pltpu.VMEM((TOK, D), BF),
            pltpu.VMEM((ROWS, 2 * KV), BF),
            dma((5,)),
        ),
    )
    block = summed_over_group(mine, other)
    block = summed_over_documents(block)
    block, grad_tokens, grad_memories = lax.optimization_barrier((block, grad_tokens, grad_memories))
    total = summed_over_segments(block) / docs
    return (grad_tokens[None], grad_memories[None, None], total[:, :KV], total[:, KV:])


def solution(mesh):
    in_specs = (
        P("dp", "seg", None),
        P("dp", "seg", None),
        P("dp", "seg", None, None),
        P("dp", None, None),
        P(),
        P("dp", None),
        P("dp", None),
        P("dp", None),
        P(None, "dp"),
    )
    out_specs = (P("dp", "seg", None), P("dp", "seg", None, None), P("dp", None), P("dp", None))
    return jax.shard_map(body, mesh=mesh, in_specs=in_specs, out_specs=out_specs, check_vma=False)
```
